128 devices in a mesh: dev: 128 (over y, x, z, core).
Axes of the slice: x: 4, y: 4, z: 4, core: 2. Of those that a mesh axis runs over, the one named last changes fastest.
Arguments:
- right_side: float32 [8192, 3, 128], P('dev'), may hold values from -105 to 105
- vertices: float32 [8192, 3, 128], P('dev'), may hold values from 0 to 1
- panels: int32 [8192, 3, 128], P('dev'), may hold values from 0 to 127
- near_owner: int32 [8192, 2], P('dev'), may hold values from 0 to 127, all different within a row; in each aligned block of 64 rows (0 to 63, 64 to 127, ...) at most 2 rows name the same one
- near_local: int32 [8192, 2], P('dev'), may hold values from 0 to 63
- far_owner: int32 [8192, 2], P('dev'), may hold values from 0 to 127, all different within a row; in each aligned block of 64 rows (0 to 63, 64 to 127, ...) at most 2 rows name the same one
- far_local: int32 [8192, 2], P('dev'), may hold values from 0 to 63
- far_left: float32 [8192, 16, 384], P('dev'), may hold values from -0.5 to 0.5
- far_right: float32 [8192, 16, 384], P('dev'), may hold values from -0.5 to 0.5
Outputs:
- krylov_basis: float32 [2, 8192, 3, 128], P(None, 'dev')
- hessenberg: float32 [3, 2], replicated
The draws below stay inside these ranges and needn't reach their ends.
Inputs may be any that keep to these rules, and one draw needn't show every extreme that they name: `near_owner`: the two entries of a row differ. Within one device's 64 rows no device number appears more than 2 times, and in every draw some number appears exactly 2 times. `far_owner`: the two entries of a row differ. Within one device's 64 rows no device number appears more than 2 times, and in every draw some number appears exactly 2 times.
All inputs are finite; a program needn't handle non-finite values.
Results may differ from the reference program's by a relative error of at most 0.0003.
Values sent between devices are 32-bit elements; how exact they have to be, the bound alone decides.
A program may use at most 64 MiB of HBM per device.

```python
import math
import jax
import jax.numpy as jnp
import numpy as np
from jax import lax

P_SIZE = 128
NV = 128
R = 16
CL_DEV = 64
NEAR_DEV = 64
FAR_DEV = 64
CAP_NEAR = 2
CAP_FAR = 2
CLUSTERS = 8192
NEAR = 8192
FAR = 8192
N_DEV = 128


def draw_right_side(key, part):
    key_value, key_row, key_col = jax.random.split(key, 3)
    position = jnp.arange(CLUSTERS, dtype=jnp.float32).reshape(CLUSTERS, 1, 1) / CLUSTERS
    row_scale = jnp.exp(jax.random.uniform(key_row, (CLUSTERS, 1, 1), jnp.float32) * math.log(10.0))
    col_scale = jnp.exp(jax.random.uniform(key_col, (1, 1, P_SIZE), jnp.float32) * math.log(10.0))
    values = jnp.clip(jax.random.normal(key_value, (CLUSTERS, 3, P_SIZE), jnp.float32), -6.0, 6.0)
    rising = 1.0 + 0.75 * position
    return values * row_scale * col_scale * rising / 10.0


def plant(entries, own_key, low, largest):
    longest = entries.shape.index(max(entries.shape))
    spots = []
    for shift in (0, 1):
        where = [jax.random.randint(jax.random.fold_in(own_key, axis), (), 0, length) for axis, length in enumerate(entries.shape)]
        where[longest] = (where[longest] + shift) % entries.shape[longest]
        spots.append(tuple(where))
    return entries.at[spots[0]].set(low).at[spots[1]].set(largest)


def block_levels(key, extent, shards, low, largest):
    def one(dim, shards_of):
        steps = jax.random.uniform(jax.random.fold_in(jax.random.fold_in(key, 6), dim), (shards_of,), jnp.float32, low / len(shards), largest / len(shards))
        return jnp.repeat(jnp.exp(steps), extent[dim] // shards_of).reshape((-1,) + (1,) * (len(extent) - dim - 1))

    loudness = one(*shards[0])
    for cut in shards[1:]:
        loudness = loudness * one(*cut)
    return loudness


def assign_block(own_key, own, number, rows, count, top, limit, skew):
    ranking = jax.random.permutation(own_key, count)
    packed, usual = shares(count, rows * top, limit, skew, True), shares(count, rows * top, limit, skew, False)
    places = jnp.arange(count)

    def named(tallies, turn):
        used = int((tallies > 0).sum())
        fixed = max(1, used // 4)
        shifted = fixed + (places - fixed + turn * (used - fixed)) % max(1, count - fixed)
        return jnp.zeros((count,), jnp.int32).at[ranking[jnp.where(places < fixed, places, shifted)]].set(jnp.asarray(tallies, jnp.int32))

    tallies = jnp.where(number % 4 == 0, named(packed, number // 4), named(usual, number - number // 4 - 1))
    mixed = jax.random.permutation(jax.random.fold_in(own, 3), count)
    donor, sink = mixed[0:count // 2 * 2:2], mixed[1:count // 2 * 2:2]
    slack = jnp.minimum(tallies[donor] - 1, limit - tallies[sink]) // 2
    slack = jnp.where((donor == ranking[0]) | (sink == ranking[0]) | (tallies[sink] == 0), 0, jnp.maximum(slack, 0))
    shifted = jax.random.randint(jax.random.fold_in(own, 4), (count // 2,), 0, 1 << 20) % (slack + 1)
    tallies = tallies.at[donor].add(-shifted).at[sink].add(shifted)
    members = jnp.searchsorted(jnp.cumsum(tallies), jnp.arange(rows * top), side="right").astype(jnp.int32)
    table = members.reshape(top, rows).T
    table = table[jax.random.permutation(jax.random.fold_in(own, 1), rows)]
    turn = jax.random.randint(jax.random.fold_in(own, 2), (rows, 1), 0, top)
    return jnp.take_along_axis(table, (jnp.arange(top)[None, :] + turn) % top, axis=1)


def shares(number_of, total, limit, slope, full):
    weights = [(1 << 20) // math.isqrt(standing ** slope) + 1 for standing in range(1, number_of + 1)]
    largest = limit if full else min(limit, max(-(-total // number_of), total * weights[0] // sum(weights)))
    least = 1 if total - largest >= number_of - 1 else 0
    given, spare = [largest] + [least] * (number_of - 1), total - largest - least * (number_of - 1)
    while spare > 0:
        candidates = [i for i in range(1, number_of) if given[i] < largest] or [i for i in range(1, number_of) if given[i] < limit]
        mass, left = sum([weights[i] for i in candidates]), spare
        for i in candidates:
            extra = min(limit - given[i], max(1, left * weights[i] // mass), spare)
            given[i] = given[i] + extra
            spare = spare - extra
    return np.array(given)


def bell_draw(key, dims, deviation, reach, cuts=(), held_as=jnp.bfloat16):
    loudness = block_levels(key, dims, cuts, -0.22, 0.18) if cuts else 1.0
    drawn = jax.random.normal(key, dims, jnp.float32) * deviation * loudness
    return jnp.minimum(jnp.maximum(drawn, -reach), reach).astype(held_as)


def setup_inputs(seed: int = 0) -> dict:
    seeds = jax.random.split(jax.random.key(seed), 10)
    right_side = draw_right_side(jax.random.fold_in(seeds[9], 71), 0)
    vertices = jnp.clip(1.0 * jax.random.uniform(seeds[1], (CLUSTERS, 3, NV), jnp.float32) ** block_levels(seeds[1], (CLUSTERS, 3, NV), ((0, 128),), -0.2, 0.2), 0.0, 1.0)
    panels = plant(jax.random.randint(seeds[2], (CLUSTERS, 3, P_SIZE), 0, NV), jax.random.fold_in(seeds[2], 1), 0, NV - 1).astype(jnp.int32)
    near_owner_keys = jax.random.split(jax.random.fold_in(seeds[3], 1), NEAR // NEAR_DEV)
    near_owner_turns = jax.random.permutation(jax.random.fold_in(seeds[3], 3), NEAR // NEAR_DEV)
    near_owner = jax.vmap(lambda own, number: assign_block(jax.random.fold_in(seeds[3], 2), own, number, NEAR_DEV, N_DEV, 2, CAP_NEAR, 2))(near_owner_keys, near_owner_turns).reshape((NEAR, 2))
    near_local = plant(jax.random.randint(seeds[4], (NEAR, 2), 0, CL_DEV), jax.random.fold_in(seeds[4], 1), 0, CL_DEV - 1).astype(jnp.int32)
    far_owner_keys = jax.random.split(jax.random.fold_in(seeds[5], 1), FAR // FAR_DEV)
    far_owner_turns = jax.random.permutation(jax.random.fold_in(seeds[5], 3), FAR // FAR_DEV)
    far_owner = jax.vmap(lambda own, number: assign_block(jax.random.fold_in(seeds[5], 2), own, number, FAR_DEV, N_DEV, 2, CAP_FAR, 2))(far_owner_keys, far_owner_turns).reshape((FAR, 2))
    far_local = plant(jax.random.randint(seeds[6], (FAR, 2), 0, CL_DEV), jax.random.fold_in(seeds[6], 1), 0, CL_DEV - 1).astype(jnp.int32)
    far_left = bell_draw(seeds[7], (FAR, R, 3 * P_SIZE), P_SIZE ** -0.5, 0.5, ((0, 128),), jnp.float32)
    far_right = bell_draw(seeds[8], (FAR, R, 3 * P_SIZE), P_SIZE ** -0.5, 0.5, ((0, 128),), jnp.float32)
    return {"right_side": right_side, "vertices": vertices, "panels": panels, "near_owner": near_owner, "near_local": near_local, "far_owner": far_owner, "far_local": far_local, "far_left": far_left, "far_right": far_right}


highest = lax.Precision.HIGHEST
soft_sq = 0.0025
area_floor = 6.25e-06
kelvin_diag = 1.8
norm_eps = 1e-06
barycentric = ((2.0 / 3.0, 1.0 / 6.0, 1.0 / 6.0), (1.0 / 6.0, 2.0 / 3.0, 1.0 / 6.0), (1.0 / 6.0, 1.0 / 6.0, 2.0 / 3.0))
index_pairs = ((0, 0), (0, 1), (0, 2), (1, 1), (1, 2), (2, 2))

def panel_corners(vertex_table, connect):
    return jnp.stack([jnp.take(vertex_table, connect[m], axis=1) for m in range(3)])

def quad_points(corners):
    edge_one = corners[1] - corners[0]
    edge_two = corners[2] - corners[0]
    cross_x = edge_one[1] * edge_two[2] - edge_one[2] * edge_two[1]
    cross_y = edge_one[2] * edge_two[0] - edge_one[0] * edge_two[2]
    cross_z = edge_one[0] * edge_two[1] - edge_one[1] * edge_two[0]
    weight = jnp.sqrt(cross_x * cross_x + cross_y * cross_y + cross_z * cross_z + area_floor) / 6.0
    points = jnp.stack([coords[0] * corners[0] + coords[1] * corners[1] + coords[2] * corners[2] for coords in barycentric])
    return (points, weight)

def near_block(points_first, weight_first, points_second, weight_second):
    panel_count = weight_first.shape[0]
    diag_sum = jnp.zeros((panel_count, panel_count), jnp.float32)
    outer_terms = [jnp.zeros((panel_count, panel_count), jnp.float32) for pair_index in index_pairs]
    for s in range(3):
        for t in range(3):
            offset = points_first[s][:, :, None] - points_second[t][:, None, :]
            inverse = lax.rsqrt(offset[0] * offset[0] + offset[1] * offset[1] + offset[2] * offset[2] + soft_sq)
            diag_sum = diag_sum + inverse
            inverse_cube = inverse * inverse * inverse
            outer_terms = [partial_sum + inverse_cube * offset[i] * offset[j] for partial_sum, (i, j) in zip(outer_terms, index_pairs)]
    weight_pair = weight_first[:, None] * weight_second[None, :]
    matrix_rows = []
    for i in range(3):
        matrix_row = []
        for j in range(3):
            entry_sum = outer_terms[index_pairs.index((min(i, j), max(i, j)))]
            if i == j:
                entry_sum = entry_sum + kelvin_diag * diag_sum
            matrix_row.append(weight_pair * entry_sum)
        matrix_rows.append(jnp.stack(matrix_row))
    return jnp.stack(matrix_rows)

def apply_near(block_matrix, dense_first, dense_second):
    into_first = jnp.einsum('ijkl,jl->ik', block_matrix, dense_second, precision=highest)
    into_second = jnp.einsum('ijkl,ik->jl', block_matrix, dense_first, precision=highest)
    return (into_first, into_second)

def apply_far(left_factors, right_factors, flat_first, flat_second):
    coef_second = jnp.einsum('frk,fk->fr', right_factors, flat_second, precision=highest)
    into_first = jnp.einsum('frk,fr->fk', left_factors, coef_second, precision=highest)
    coef_first = jnp.einsum('frk,fk->fr', left_factors, flat_first, precision=highest)
    into_second = jnp.einsum('frk,fr->fk', right_factors, coef_first, precision=highest)
    return (into_first, into_second)

def reference(right_side, vertices, panels, near_owner, near_local, far_owner, far_local, far_left, far_right):
    corners = jax.vmap(panel_corners)(vertices, panels)
    points, weights = jax.vmap(quad_points)(corners)
    near_ids = (near_owner * CL_DEV + near_local).astype(jnp.int32)
    far_ids = (far_owner * CL_DEV + far_local).astype(jnp.int32)
    size_all = CLUSTERS * 3 * P_SIZE

    def product(density):

        def near_step(image_sum, pair_ids):
            ids_first = pair_ids[:, 0]
            ids_second = pair_ids[:, 1]
            blocks = jax.vmap(near_block)(points[ids_first], weights[ids_first], points[ids_second], weights[ids_second])
            into_first, into_second = jax.vmap(apply_near)(blocks, density[ids_first], density[ids_second])
            image_sum = image_sum.at[ids_first].add(into_first).at[ids_second].add(into_second)
            return (image_sum, None)
        image_sum, unused_out = lax.scan(near_step, jnp.zeros((CLUSTERS, 3, P_SIZE), jnp.float32), near_ids.reshape(N_DEV * NEAR_DEV // 4, 4, 2))
        flat_density = density.reshape(CLUSTERS, 3 * P_SIZE)
        far_first, far_second = apply_far(far_left, far_right, flat_density[far_ids[:, 0]], flat_density[far_ids[:, 1]])
        image_sum = image_sum.reshape(CLUSTERS, 3 * P_SIZE).at[far_ids[:, 0]].add(far_first).at[far_ids[:, 1]].add(far_second)
        return image_sum.reshape(CLUSTERS, 3, P_SIZE)

    def mean_inner(left_vec, right_vec):
        return jnp.sum(left_vec * right_vec) / size_all
    rhs_scale = jnp.sqrt(mean_inner(right_side, right_side) + norm_eps)
    basis_one = right_side / rhs_scale
    image_one = product(basis_one)
    proj_first = mean_inner(basis_one, image_one)
    resid_one = image_one - proj_first * basis_one
    norm_first = jnp.sqrt(mean_inner(resid_one, resid_one) + norm_eps)
    basis_two = resid_one / norm_first
    image_two = product(basis_two)
    proj_cross = mean_inner(basis_one, image_two)
    proj_second = mean_inner(basis_two, image_two)
    resid_two = image_two - proj_cross * basis_one - proj_second * basis_two
    norm_second = jnp.sqrt(mean_inner(resid_two, resid_two) + norm_eps)
    basis_three = resid_two / norm_second
    zero_entry = jnp.zeros((), jnp.float32)
    hessenberg = jnp.stack([jnp.stack([proj_first, proj_cross]), jnp.stack([norm_first, proj_second]), jnp.stack([zero_entry, norm_second])])
    return (jnp.stack([basis_two, basis_three]), hessenberg)
```

```python
import functools

import jax
import jax.numpy as jnp
from jax import lax
from jax.experimental import pallas as pl
from jax.experimental.pallas import tpu as pltpu
from jax.sharding import PartitionSpec as P

highest = lax.Precision.HIGHEST
soft_sq = 0.0025
area_floor = 6.25e-06
kelvin_diag = 1.8
norm_eps = 1e-06
lanes = 128
f32 = jnp.float32
i32 = jnp.int32
mesh_id = pl.DeviceIdType.MESH


def list_tables(owner_row, local_row):
    shape = (lanes, lanes)
    sub = lax.broadcasted_iota(i32, shape, 0)
    lane = lax.broadcasted_iota(i32, shape, 1)
    sub_f = sub.astype(f32)
    lane_f = lane.astype(f32)
    owner_b = jnp.broadcast_to(owner_row, shape)
    owner_t = owner_b.T
    local_t = jnp.broadcast_to(local_row, shape).T
    same = owner_b == owner_t
    rank_row = jnp.sum(jnp.where(same & (sub < lane), 1.0, 0.0), axis=0, keepdims=True)
    rank_col = jnp.sum(jnp.where(same & (lane < sub), 1.0, 0.0), axis=1, keepdims=True)
    slot_row = owner_row * 2.0 + rank_row
    requests, entries = [], []
    for k in range(2):
        hit = (owner_t == lane_f) & (rank_col == float(k))
        requests.append(jnp.sum(jnp.where(hit, local_t, 0.0), axis=0, keepdims=True))
        entries.append(
            jnp.sum(jnp.where(hit, sub_f - float(lanes), 0.0), axis=0, keepdims=True) + float(lanes)
        )
    return slot_row, requests, entries


def kernel(
    n,
    near,
    far,
    index_ref,
    x_ref,
    vert_ref,
    panel_ref,
    left_ref,
    right_ref,
    basis_ref,
    hess_ref,
    req_send,
    req_recv,
    tab_v,
    tab_s,
    ask_v,
    ask_s,
    one_hot,
    panel_f,
    geo_send,
    geo_recv,
    x_send,
    x_recv,
    y_send,
    y_recv,
    near_send,
    near_recv,
    far_send,
    far_recv,
    points,
    points_t,
    blocks,
    first_rows,
    first_cols,
    out_cols,
    near_terms,
    far_terms,
    y_here,
    z_here,
    sum_send,
    sum_recv,
    send_sem,
    recv_sem,
    local_sem,
):
    me = lax.axis_index("dev")
    clusters = x_ref.shape[0]
    size_all = float(clusters * n * 3 * lanes)

    barrier = pltpu.get_barrier_semaphore()

    def greet(i, carry):
        pl.semaphore_signal(
            barrier, inc=1, device_id=(lax.rem(me + i, n),), device_id_type=mesh_id
        )
        return carry

    lax.fori_loop(1, n, greet, 0)

    def asked_id(k, o):
        return jnp.clip(ask_s[k, o], 0, clusters - 1)

    def entry_slot(row, e):
        slot = jnp.clip(tab_s[row, e], 0, 2 * n - 1)
        return slot >> 1, slot & 1

    index_rows = index_ref[...].astype(f32)
    near_slot, near_req, near_entry = list_tables(index_rows[0:1], index_rows[1:2])
    far_slot, far_req, far_entry = list_tables(index_rows[2:3], index_rows[3:4])
    rows = [near_slot, far_slot] + near_entry + far_entry
    tab_v[...] = jnp.concatenate(rows + [jnp.zeros((2, lanes), f32)], axis=0).astype(i32)
    to_smem = pltpu.make_async_copy(tab_v, tab_s, local_sem.at[0])
    to_smem.start()
    req_rows = jnp.concatenate(near_req + far_req + [jnp.zeros((lanes - 4, lanes), f32)], axis=0)
    req_send[...] = req_rows.T[:n].reshape(n, 1, lanes)
    panel_f[...] = panel_ref[...].astype(f32)
    near_terms[pl.ds(4 * lanes, 8), :] = jnp.zeros((8, lanes), f32)
    far_terms[pl.ds(4 * lanes, 8), :] = jnp.zeros((8, lanes), f32)
    out_cols[...] = jnp.zeros(out_cols.shape, f32)

    pl.semaphore_wait(barrier, n - 1)

    def exchange(send, recv, which, fill):
        fill(me)
        pltpu.make_async_copy(send.at[me], recv.at[me], recv_sem.at[which]).start()

        def step(i, carry):
            peer = lax.rem(me + i, n)
            fill(peer)
            pltpu.make_async_remote_copy(
                send.at[peer],
                recv.at[me],
                send_sem.at[which],
                recv_sem.at[which],
                device_id=(peer,),
                device_id_type=mesh_id,
            ).start()
            return carry

        lax.fori_loop(1, n, step, 0)

    def arrived(recv, which):
        pltpu.make_async_copy(recv, recv, recv_sem.at[which]).wait()

    def sent(send, which):
        part = send.at[pl.ds(0, n - 1)]
        pltpu.make_async_copy(part, part, send_sem.at[which]).wait()

    exchange(req_send, req_recv, 0, lambda o: None)
    arrived(req_recv, 0)
    asked = req_recv[...].reshape(n, lanes)
    if n < lanes:
        asked = jnp.concatenate([asked, jnp.zeros((lanes - n, lanes), f32)], axis=0)
    asked = asked.T
    ask_v[...] = asked[0:8].astype(i32)
    ask_copy = pltpu.make_async_copy(ask_v, ask_s, local_sem.at[1])
    ask_copy.start()
    cluster_ids = lax.broadcasted_iota(i32, (clusters, lanes), 0).astype(f32)
    for k in range(4):
        one_hot[k] = jnp.where(cluster_ids == asked[k : k + 1], 1.0, 0.0)
    ask_copy.wait()
    to_smem.wait()

    def fill_geo(o):
        for k in range(2):
            c = asked_id(k, o)
            geo_send[o, k, 0] = vert_ref[c]
            geo_send[o, k, 1] = panel_f[c]

    def fill_density(send, source):
        def fill(o):
            for k in range(4):
                send[o, k] = source[asked_id(k, o)]

        return fill

    exchange(geo_send, geo_recv, 1, fill_geo)
    exchange(x_send, x_recv, 2, fill_density(x_send, x_ref))
    arrived(geo_recv, 1)

    def make_points(p, carry):
        owner_a, rank_a = entry_slot(0, p)
        owner_b, rank_b = entry_slot(0, near + p)
        va = geo_recv[owner_a, rank_a, 0]
        vb = geo_recv[owner_b, rank_b, 0]
        pa = geo_recv[owner_a, rank_a, 1].astype(i32)
        pb = geo_recv[owner_b, rank_b, 1].astype(i32)
        table = jnp.concatenate([va, va[0:1], vb, vb[0:1]], axis=0)
        corners = []
        for m in range(3):
            picks = jnp.concatenate(
                [
                    jnp.broadcast_to(pa[m : m + 1], (4, lanes)),
                    jnp.broadcast_to(pb[m : m + 1], (4, lanes)),
                ],
                axis=0,
            )
            corners.append(
                jnp.take_along_axis(table, picks, axis=1, mode="promise_in_bounds")
            )
        edge_one = corners[1] - corners[0]
        edge_two = corners[2] - corners[0]
        cross = edge_one * pltpu.roll(edge_two, 7, 0) - pltpu.roll(edge_one, 7, 0) * edge_two
        squares = cross * cross
        area = squares + pltpu.roll(squares, 7, 0) + pltpu.roll(squares, 6, 0)
        weight = jnp.sqrt(area + area_floor) / 6.0
        for s in range(3):
            others = [corners[m] for m in range(3) if m != s]
            points[p, s] = (2.0 / 3.0) * corners[s] + (1.0 / 6.0) * (others[0] + others[1])
        points[p, 3] = weight
        return carry

    lax.fori_loop(0, near, make_points, 0)

    def turn_points(g, carry):
        points_t[g] = points[pl.ds(4 * g, 4)].reshape(lanes, lanes).T
        return carry

    lax.fori_loop(0, near // 4, turn_points, 0)

    chunk = 16

    def make_block(p, carry):
        group = p // 4
        shift = lanes - (p % 4) * 32
        for c in range(lanes // chunk):
            at = pltpu.roll(points_t[group, pl.ds(c * chunk, chunk), :], shift, 1)
            inv_sum = jnp.zeros((chunk, lanes), f32)
            cube_sum = jnp.zeros((chunk, lanes), f32)
            outer = [jnp.zeros((chunk, lanes), f32) for _ in range(5)]
            for s in range(3):
                a = [at[:, 8 * s + i : 8 * s + i + 1] for i in range(3)]
                for t in range(3):
                    d = [a[i] - points[p, t, 4 + i : 5 + i, :] for i in range(3)]
                    inv = lax.rsqrt(d[0] * d[0] + d[1] * d[1] + (d[2] * d[2] + soft_sq))
                    cube = inv * inv * inv
                    e0 = cube * d[0]
                    e1 = cube * d[1]
                    inv_sum = inv_sum + inv
                    cube_sum = cube_sum + cube
                    outer = [
                        outer[0] + e0 * d[0],
                        outer[1] + e0 * d[1],
                        outer[2] + e0 * d[2],
                        outer[3] + e1 * d[1],
                        outer[4] + e1 * d[2],
                    ]
            weight = at[:, 24:25] * points[p, 3, 4:5, :]
            last = inv_sum - soft_sq * cube_sum - outer[0] - outer[3]
            diag = kelvin_diag * inv_sum
            at_rows = pl.ds(c * chunk, chunk)
            blocks[p, 0, at_rows, :] = weight * (outer[0] + diag)
            blocks[p, 1, at_rows, :] = weight * outer[1]
            blocks[p, 2, at_rows, :] = weight * outer[2]
            blocks[p, 3, at_rows, :] = weight * (outer[3] + diag)
            blocks[p, 4, at_rows, :] = weight * outer[4]
            blocks[p, 5, at_rows, :] = weight * (last + diag)
        return carry

    pair_at = ((0, 1, 2), (1, 3, 4), (2, 4, 5))

    def apply_far(recv):
        def step(f, carry):
            owner_a, rank_a = entry_slot(1, f)
            owner_b, rank_b = entry_slot(1, far + f)
            xa = recv[owner_a, 2 + rank_a]
            xb = recv[owner_b, 2 + rank_b]
            left = [left_ref[f, :, pl.ds(c * lanes, lanes)] for c in range(3)]
            right = [right_ref[f, :, pl.ds(c * lanes, lanes)] for c in range(3)]
            coef_b = jnp.sum(
                right[0] * xb[0:1] + right[1] * xb[1:2] + right[2] * xb[2:3], axis=1, keepdims=True
            )
            coef_a = jnp.sum(
                left[0] * xa[0:1] + left[1] * xa[1:2] + left[2] * xa[2:3], axis=1, keepdims=True
            )
            for c in range(3):
                far_terms[pl.ds(4 * f + c, 1), :] = jnp.sum(left[c] * coef_b, axis=0, keepdims=True)
                far_terms[pl.ds(4 * (far + f) + c, 1), :] = jnp.sum(
                    right[c] * coef_a, axis=0, keepdims=True
                )
            return carry

        lax.fori_loop(0, far, step, 0)

    per_tile = lanes // 4
    tiles = -(-near // per_tile)

    def apply_near(recv):
        def gather(h, carry):
            parts = []
            for q in range(2):
                owner, rank = entry_slot(0, 2 * h + q)
                rows_q = recv[owner, rank]
                parts += [rows_q, rows_q[0:1]]
            first_rows[pl.ds(pl.multiple_of(8 * h, 8), 8), :] = jnp.concatenate(parts, axis=0)
            return carry

        lax.fori_loop(0, near // 2, gather, 0)
        for g in range(tiles):
            first_cols[g] = first_rows[pl.ds(g * lanes, lanes), :].T
        lane_ids = lax.broadcasted_iota(i32, (chunk, lanes), 1)

        def step(p, carry):
            group = p // per_tile
            base = 4 * (p % per_tile)
            owner_b, rank_b = entry_slot(0, near + p)
            xb = recv[owner_b, rank_b]
            into = [jnp.zeros((chunk, lanes), f32) for _ in range(3)]
            for c in range(lanes // chunk):
                at_rows = pl.ds(c * chunk, chunk)
                cols = pltpu.roll(first_cols[group, at_rows, :], lanes - base, 1)
                mats = [blocks[p, q, at_rows, :] for q in range(6)]
                kept = out_cols[group, at_rows, :]
                for i in range(3):
                    m = [mats[q] for q in pair_at[i]]
                    summed = jnp.sum(
                        m[0] * xb[0:1] + m[1] * xb[1:2] + m[2] * xb[2:3], axis=1, keepdims=True
                    )
                    kept = jnp.where(lane_ids == base + i, summed, kept)
                    xa = cols[:, i : i + 1]
                    into = [into[j] + m[j] * xa for j in range(3)]
                out_cols[group, at_rows, :] = kept
            for j in range(3):
                near_terms[pl.ds(4 * (near + p) + j, 1), :] = jnp.sum(
                    into[j], axis=0, keepdims=True
                )
            return carry

        lax.fori_loop(0, near, step, 0)
        for g in range(tiles):
            count = min(lanes, 4 * near - g * lanes)
            near_terms[pl.ds(g * lanes, count), :] = out_cols[g].T[:count]

    def fill_terms(send, source, row):
        def fill(o):
            for k in range(2):
                entry = jnp.clip(tab_s[row + k, o], 0, lanes)
                send[o, k] = source[pl.ds(4 * entry, 3), :]

        return fill

    def reduce_terms(stage, target):
        for c in range(3):
            total = jnp.zeros((clusters, lanes), f32)
            for k in range(2):
                total = total + jnp.dot(
                    one_hot[k, :, pl.ds(0, n)],
                    near_recv[stage, :, k, c, :],
                    precision=highest,
                    preferred_element_type=f32,
                )
                total = total + jnp.dot(
                    one_hot[2 + k, :, pl.ds(0, n)],
                    far_recv[stage, :, k, c, :],
                    precision=highest,
                    preferred_element_type=f32,
                )
            target[:, c, :] = total

    def mean_of(u, v):
        return jnp.sum(jnp.sum(u * v, axis=0), keepdims=True) * (1.0 / size_all)

    def send_sums(which, values):
        lane_row = lax.broadcasted_iota(i32, (1, lanes), 1)
        row = jnp.zeros((1, lanes), f32)
        for j, value in enumerate(values):
            row = jnp.where(lane_row == j, value, row)
        sum_send[which] = row
        pltpu.make_async_copy(
            sum_send.at[which], sum_recv.at[which, me], recv_sem.at[7 + which]
        ).start()

        def step(i, carry):
            peer = lax.rem(me + i, n)
            pltpu.make_async_remote_copy(
                sum_send.at[which],
                sum_recv.at[which, me],
                send_sem.at[7 + which],
                recv_sem.at[7 + which],
                device_id=(peer,),
                device_id_type=mesh_id,
            ).start()
            return carry

        lax.fori_loop(1, n, step, 0)

    def take_sums(which, count):
        arrived(sum_recv.at[which], 7 + which)
        total = jnp.sum(sum_recv[which], axis=0)
        return [total[0:1, j : j + 1] for j in range(count)]

    half = near // 2
    lax.fori_loop(0, half, make_block, 0)
    arrived(x_recv, 2)
    apply_far(x_recv)
    exchange(far_send.at[0], far_recv.at[0], 3, fill_terms(far_send.at[0], far_terms, 4))
    lax.fori_loop(half, near, make_block, 0)
    apply_near(x_recv)
    exchange(near_send.at[0], near_recv.at[0], 4, fill_terms(near_send.at[0], near_terms, 2))
    arrived(far_recv.at[0], 3)
    arrived(near_recv.at[0], 4)
    reduce_terms(0, y_here)

    exchange(y_send, y_recv, 9, fill_density(y_send, y_here))
    x = x_ref[...]
    y = y_here[...]
    send_sums(0, [mean_of(x, x), mean_of(x, y), mean_of(y, y)])
    arrived(y_recv, 9)
    apply_far(y_recv)
    exchange(far_send.at[1], far_recv.at[1], 5, fill_terms(far_send.at[1], far_terms, 4))
    apply_near(y_recv)
    exchange(near_send.at[1], near_recv.at[1], 6, fill_terms(near_send.at[1], near_terms, 2))
    xx, xy, yy = take_sums(0, 3)
    scale_sq = xx + norm_eps
    scale = jnp.sqrt(scale_sq)
    proj_first = xy / scale_sq
    resid_sq = (yy - proj_first * xy * (1.0 + norm_eps / scale_sq)) / scale_sq
    norm_sq = resid_sq + norm_eps
    norm_first = jnp.sqrt(norm_sq)
    shrink = 1.0 / (scale * norm_first)
    x = x_ref[...]
    y = y_here[...]
    basis_one = x / scale
    basis_two = (y - proj_first * x) * shrink
    basis_ref[0] = basis_two
    arrived(far_recv.at[1], 5)
    arrived(near_recv.at[1], 6)
    reduce_terms(1, z_here)
    image_two = (z_here[...] - proj_first * y_here[...]) * shrink
    send_sums(
        1, [mean_of(basis_one, image_two), mean_of(basis_two, image_two), mean_of(image_two, image_two)]
    )
    cross, second, image_sq = take_sums(1, 3)
    one_sq = xx / scale_sq
    two_sq = resid_sq / norm_sq
    one_two = xy * norm_eps / (scale_sq * scale_sq * norm_first)
    last_sq = (
        image_sq
        + cross * cross * (one_sq - 2.0)
        + second * second * (two_sq - 2.0)
        + 2.0 * cross * second * one_two
    )
    norm_second = jnp.sqrt(last_sq + norm_eps)
    shrink_two = 1.0 / norm_second
    basis_ref[1] = (image_two - cross * basis_one - second * basis_two) * shrink_two
    row_id = lax.broadcasted_iota(i32, (3, 2), 0)
    col_id = lax.broadcasted_iota(i32, (3, 2), 1)
    hess = jnp.zeros((3, 2), f32)
    placed = (
        (0, 0, proj_first),
        (0, 1, cross),
        (1, 0, norm_first),
        (1, 1, second),
        (2, 1, norm_second),
    )
    for r, c, value in placed:
        hess = jnp.where((row_id == r) & (col_id == c), value, hess)
    hess_ref[...] = hess

    sent(req_send, 0)
    sent(geo_send, 1)
    sent(x_send, 2)
    sent(far_send.at[0], 3)
    sent(near_send.at[0], 4)
    sent(far_send.at[1], 5)
    sent(near_send.at[1], 6)
    sent(y_send, 9)
    for which in range(2):
        sent(sum_recv.at[which], 7 + which)


def per_device(
    right_side, vertices, panels, near_owner, near_local, far_owner, far_local, far_left, far_right
):
    n = lax.axis_size("dev")
    near = near_owner.shape[0]
    far = far_owner.shape[0]
    clusters = right_side.shape[0]

    def entry_row(table, fill):
        row = table.T.reshape(1, -1)
        return jnp.pad(row, ((0, 0), (0, lanes - row.shape[1])), constant_values=fill)

    index = jnp.concatenate(
        [
            entry_row(near_owner, -1),
            entry_row(near_local, 0),
            entry_row(far_owner, -1),
            entry_row(far_local, 0),
        ]
        * 2,
        axis=0,
    )
    tiles = -(-4 * near // lanes)
    vmem = pltpu.VMEM
    return pl.pallas_call(
        functools.partial(kernel, n, near, far),
        out_shape=(
            jax.ShapeDtypeStruct((2, clusters, 3, lanes), f32),
            jax.ShapeDtypeStruct((3, 2), f32),
        ),
        in_specs=[pl.BlockSpec(memory_space=vmem)] * 6,
        out_specs=(pl.BlockSpec(memory_space=vmem),) * 2,
        scratch_shapes=[
            vmem((n, 1, lanes), f32),
            vmem((n, 1, lanes), f32),
            vmem((8, lanes), i32),
            pltpu.SMEM((8, lanes), i32),
            vmem((8, lanes), i32),
            pltpu.SMEM((8, lanes), i32),
            vmem((4, clusters, lanes), f32),
            vmem((clusters, 3, lanes), f32),
            vmem((n, 2, 2, 3, lanes), f32),
            vmem((n, 2, 2, 3, lanes), f32),
            vmem((n, 4, 3, lanes), f32),
            vmem((n, 4, 3, lanes), f32),
            vmem((n, 4, 3, lanes), f32),
            vmem((n, 4, 3, lanes), f32),
            vmem((2, n, 2, 3, lanes), f32),
            vmem((2, n, 2, 3, lanes), f32),
            vmem((2, n, 2, 3, lanes), f32),
            vmem((2, n, 2, 3, lanes), f32),
            vmem((near, 4, 8, lanes), f32),
            vmem((near // 4, lanes, lanes), f32),
            vmem((near, 6, lanes, lanes), f32),
            vmem((tiles * lanes, lanes), f32),
            vmem((tiles, lanes, lanes), f32),
            vmem((tiles, lanes, lanes), f32),
            vmem((4 * lanes + 8, lanes), f32),
            vmem((4 * lanes + 8, lanes), f32),
            vmem((clusters, 3, lanes), f32),
            vmem((clusters, 3, lanes), f32),
            vmem((2, 1, lanes), f32),
            vmem((2, n, 1, lanes), f32),
            pltpu.SemaphoreType.DMA((10,)),
            pltpu.SemaphoreType.DMA((10,)),
            pltpu.SemaphoreType.DMA((2,)),
        ],
        compiler_params=pltpu.CompilerParams(
            collective_id=0, has_side_effects=True, vmem_limit_bytes=58 * 1024 * 1024
        ),
    )(index, right_side, vertices, panels, far_left, far_right)


def solution(mesh):
    block = P("dev", None, None)
    pair = P("dev", None)
    return jax.shard_map(
        per_device,
        mesh=mesh,
        in_specs=(block, block, block, pair, pair, pair, pair, block, block),
        out_specs=(P(None, "dev", None, None), P()),
        check_vma=False,
    )
```

```python
import functools

import jax
import jax.numpy as jnp
from jax import lax
from jax.experimental import pallas as pl
from jax.experimental.pallas import tpu as pltpu
from jax.sharding import PartitionSpec as P

highest = lax.Precision.HIGHEST
soft_sq = 0.0025
area_floor = 6.25e-06
kelvin_diag = 1.8
norm_eps = 1e-06
lanes = 128
f32 = jnp.float32
i32 = jnp.int32
bf16 = jnp.bfloat16
mesh_id = pl.DeviceIdType.MESH


def list_tables(owners, locals_, count):
    owner_row = jnp.concatenate([owners[0:1], owners[1:2]], axis=1).astype(f32)
    local_row = jnp.concatenate([locals_[0:1], locals_[1:2]], axis=1).astype(f32)
    shape = (lanes, lanes)
    sub = lax.broadcasted_iota(i32, shape, 0)
    lane = lax.broadcasted_iota(i32, shape, 1)
    tile = (2 * (sub % count) + sub // count - lanes).astype(f32)
    lane_f = lane.astype(f32)
    owner_b = jnp.broadcast_to(owner_row, shape)
    owner_t = owner_b.T
    local_t = jnp.broadcast_to(local_row, shape).T
    same = owner_b == owner_t
    rank_row = jnp.sum(jnp.where(same & (sub < lane), 1.0, 0.0), axis=0, keepdims=True)
    rank_col = jnp.sum(jnp.where(same & (lane < sub), 1.0, 0.0), axis=1, keepdims=True)
    slot_row = owner_row * 2.0 + rank_row
    requests, entries = [], []
    for k in range(2):
        hit = (owner_t == lane_f) & (rank_col == float(k))
        requests.append(jnp.sum(jnp.where(hit, local_t, 0.0), axis=0, keepdims=True))
        entries.append(
            jnp.sum(jnp.where(hit, tile, 0.0), axis=0, keepdims=True) + float(lanes)
        )
    return slot_row, requests, entries


def three_parts(rows):
    high = rows.astype(bf16).astype(f32)
    rest = rows - high
    middle = rest.astype(bf16).astype(f32)
    return [high, middle, rest - middle]


def kernel(
    n,
    near,
    far,
    near_owner_ref,
    near_local_ref,
    far_owner_ref,
    far_local_ref,
    x_ref,
    vert_ref,
    panel_ref,
    left_ref,
    right_ref,
    basis_ref,
    hess_ref,
    req_send,
    req_recv,
    tab_v,
    tab_s,
    ask_v,
    ask_s,
    one_hot,
    x_here,
    vert_here,
    panel_here,
    geo_send,
    geo_recv,
    x_send,
    x_recv,
    yn_send,
    yn_recv,
    yf_send,
    yf_recv,
    near_send,
    near_recv,
    far_send,
    far_recv,
    points,
    first_rows,
    first_cols,
    picker,
    cols_even,
    cols_odd,
    blocks_0,
    blocks_1,
    blocks_2,
    blocks_3,
    near_terms,
    far_terms,
    y_all,
    z_all,
    y_here,
    sum_send,
    sum_recv,
    send_sem,
    recv_sem,
    local_sem,
):
    me = lax.axis_index("dev")
    clusters = x_ref.shape[1]
    blocks = (blocks_0, blocks_1, blocks_2, blocks_3)
    size_all = float(clusters * n * 3 * lanes)

    barrier = pltpu.get_barrier_semaphore()

    def greet(i, carry):
        pl.semaphore_signal(
            barrier, inc=1, device_id=(lax.rem(me + i, n),), device_id_type=mesh_id
        )
        return carry

    lax.fori_loop(1, n, greet, 0)

    def asked_id(k, o):
        return jnp.clip(ask_s[k, o], 0, clusters - 1)

    def entry_slot(row, e):
        slot = jnp.clip(tab_s[row, e], 0, 2 * n - 1)
        return slot >> 1, slot & 1

    near_slot, near_req, near_entry = list_tables(near_owner_ref[...], near_local_ref[...], near)
    far_slot, far_req, far_entry = list_tables(far_owner_ref[...], far_local_ref[...], far)
    rows = [near_slot, far_slot] + near_entry + far_entry
    tab_v[...] = jnp.concatenate(rows + [jnp.zeros((2, lanes), f32)], axis=0).astype(i32)
    to_smem = pltpu.make_async_copy(tab_v, tab_s, local_sem.at[0])
    to_smem.start()
    req_rows = jnp.concatenate(near_req + far_req + [jnp.zeros((lanes - 4, lanes), f32)], axis=0)
    req_send[...] = req_rows.T[:n].reshape(n, 1, lanes)
    for c in range(3):
        x_here[:, c, :] = x_ref[c]
        vert_here[:, c, :] = vert_ref[c]
        panel_here[:, c, :] = panel_ref[c].astype(f32)
    near_terms[pl.ds(4 * lanes, 8), :] = jnp.zeros((8, lanes), f32)
    far_terms[pl.ds(4 * lanes, 8), :] = jnp.zeros((8, lanes), f32)

    picked = lax.broadcasted_iota(i32, (lanes, lanes), 0)
    for r in range(4):
        for j in range(9):
            place = picked - 32 * r
            if j < 8:
                hit = (place == j) | (place == 8 + j) | (place == 16 + j)
            else:
                hit = (place >= 24) & (place < 27)
            picker[r, :, pl.ds(j * lanes, lanes)] = jnp.where(hit, 1.0, 0.0).astype(bf16)

    pl.semaphore_wait(barrier, n - 1)

    def exchange(send, recv, which, fill):
        fill(me)
        pltpu.make_async_copy(send.at[me], recv.at[me], recv_sem.at[which]).start()

        def step(i, carry):
            peer = lax.rem(me + i, n)
            fill(peer)
            pltpu.make_async_remote_copy(
                send.at[peer],
                recv.at[me],
                send_sem.at[which],
                recv_sem.at[which],
                device_id=(peer,),
                device_id_type=mesh_id,
            ).start()
            return carry

        lax.fori_loop(1, n, step, 0)

    def arrived(recv, which):
        pltpu.make_async_copy(recv, recv, recv_sem.at[which]).wait()

    def sent(send, which):
        part = send.at[pl.ds(0, n - 1)]
        pltpu.make_async_copy(part, part, send_sem.at[which]).wait()

    exchange(req_send, req_recv, 0, lambda o: None)
    arrived(req_recv, 0)
    asked = req_recv[...].reshape(n, lanes)
    if n < lanes:
        asked = jnp.concatenate([asked, jnp.zeros((lanes - n, lanes), f32)], axis=0)
    asked = asked.T
    ask_v[...] = asked[0:8].astype(i32)
    ask_copy = pltpu.make_async_copy(ask_v, ask_s, local_sem.at[1])
    ask_copy.start()
    cluster_ids = lax.broadcasted_iota(i32, (clusters, lanes), 0).astype(f32)
    for k in range(4):
        one_hot[k] = jnp.where(cluster_ids == asked[k : k + 1], 1.0, 0.0)
    ask_copy.wait()
    to_smem.wait()

    def fill_geo(o):
        for k in range(2):
            c = asked_id(k, o)
            geo_send[o, k, 0] = vert_here[c]
            geo_send[o, k, 1] = panel_here[c]

    def fill_density(send, source, slots):
        def fill(o):
            for j, k in enumerate(slots):
                send[o, j] = source[asked_id(k, o)]

        return fill

    exchange(geo_send, geo_recv, 1, fill_geo)
    exchange(x_send, x_recv, 2, fill_density(x_send, x_here, (0, 1, 2, 3)))
    arrived(geo_recv, 1)

    def make_points(p):
        owner_a, rank_a = entry_slot(0, p)
        owner_b, rank_b = entry_slot(0, near + p)
        va = geo_recv[owner_a, rank_a, 0]
        vb = geo_recv[owner_b, rank_b, 0]
        pa = geo_recv[owner_a, rank_a, 1].astype(i32)
        pb = geo_recv[owner_b, rank_b, 1].astype(i32)
        table = jnp.concatenate([va, va[0:1], vb, vb[0:1]], axis=0)
        corners = []
        for m in range(3):
            picks = jnp.concatenate(
                [
                    jnp.broadcast_to(pa[m : m + 1], (4, lanes)),
                    jnp.broadcast_to(pb[m : m + 1], (4, lanes)),
                ],
                axis=0,
            )
            corners.append(
                jnp.take_along_axis(table, picks, axis=1, mode="promise_in_bounds")
            )
        edge_one = corners[1] - corners[0]
        edge_two = corners[2] - corners[0]
        cross = edge_one * pltpu.roll(edge_two, 7, 0) - pltpu.roll(edge_one, 7, 0) * edge_two
        squares = cross * cross
        area = squares + pltpu.roll(squares, 7, 0) + pltpu.roll(squares, 6, 0)
        weight = jnp.sqrt(area + area_floor) / 6.0
        for s in range(3):
            others = [corners[m] for m in range(3) if m != s]
            points[p, s] = (2.0 / 3.0) * corners[s] + (1.0 / 6.0) * (others[0] + others[1])
        points[p, 3] = weight
        firsts = [points[p, s] for s in range(3)]
        head = jnp.concatenate([firsts[0][0:3], firsts[1][0:3], firsts[2][0:2]], axis=0)
        head_parts, tail_parts = three_parts(head), three_parts(firsts[2])
        first_rows[pl.ds(pl.multiple_of(32 * p, 32), 32), :] = jnp.concatenate(
            head_parts + [part[2:3] for part in tail_parts] + [jnp.zeros((5, lanes), f32)], axis=0
        )

    def points_step(h, carry):
        for u in range(4):
            make_points(4 * h + u)
        return carry

    lax.fori_loop(0, near // 4, points_step, 0)

    def turn_points(g, carry):
        rows = first_rows[pl.ds(pl.multiple_of(lanes * g, lanes), lanes), :]
        first_cols[g] = rows.T.astype(bf16)
        return carry

    lax.fori_loop(0, near // 4, turn_points, 0)

    chunk = 16

    def spread_first(p, target):
        target[...] = jnp.dot(first_cols[p // 4], picker[p % 4], preferred_element_type=f32)

    def make_block(p, cols, target, at):
        for c in range(lanes // chunk):
            at_rows = pl.ds(c * chunk, chunk)
            inv_sum = jnp.zeros((chunk, lanes), f32)
            cube_sum = jnp.zeros((chunk, lanes), f32)
            outer = [jnp.zeros((chunk, lanes), f32) for _ in range(5)]
            for s in range(3):
                a = [cols[at_rows, pl.ds((3 * s + i) * lanes, lanes)] for i in range(3)]
                for t in range(3):
                    d = [a[i] - points[p, t, 4 + i : 5 + i, :] for i in range(3)]
                    inv = lax.rsqrt(d[0] * d[0] + d[1] * d[1] + (d[2] * d[2] + soft_sq))
                    cube = inv * inv * inv
                    e0 = cube * d[0]
                    e1 = cube * d[1]
                    inv_sum = inv_sum + inv
                    cube_sum = cube_sum + cube
                    outer = [
                        outer[0] + e0 * d[0],
                        outer[1] + e0 * d[1],
                        outer[2] + e0 * d[2],
                        outer[3] + e1 * d[1],
                        outer[4] + e1 * d[2],
                    ]
            last = inv_sum - soft_sq * cube_sum - outer[0] - outer[3]
            diag = kelvin_diag * inv_sum
            entries = (
                outer[0] + diag,
                outer[1],
                outer[2],
                outer[3] + diag,
                outer[4],
                last + diag,
            )
            for q in range(6):
                value = entries[q]
                high = value.astype(bf16)
                at_lanes = pl.ds(q * lanes, lanes)
                target[at, at_rows, at_lanes] = high
                target[at, pl.ds(lanes + c * chunk, chunk), at_lanes] = (
                    value - high.astype(f32)
                ).astype(bf16)

    quarter = near // 4

    def make_quarter(k, recv):
        def step(h, carry):
            at = 2 * h
            p = k * quarter + at
            spread_first(p + 1, cols_odd)
            if recv is not None:
                near_pair(recv, p - quarter, blocks[k - 1], at)
            make_block(p, cols_even, blocks[k], at)
            spread_first(jnp.minimum(p + 2, near - 1), cols_even)
            if recv is not None:
                near_pair(recv, p + 1 - quarter, blocks[k - 1], at + 1)
            make_block(p + 1, cols_odd, blocks[k], at + 1)
            return carry

        lax.fori_loop(0, quarter // 2, step, 0)

    def apply_far(recv, base):
        def one(f):
            owner_a, rank_a = entry_slot(1, f)
            owner_b, rank_b = entry_slot(1, far + f)
            xa = recv[owner_a, base + rank_a]
            xb = recv[owner_b, base + rank_b]
            left = [left_ref[f, :, pl.ds(c * lanes, lanes)] for c in range(3)]
            right = [right_ref[f, :, pl.ds(c * lanes, lanes)] for c in range(3)]
            coef_b = jnp.sum(
                right[0] * xb[0:1] + right[1] * xb[1:2] + right[2] * xb[2:3], axis=1, keepdims=True
            )
            coef_a = jnp.sum(
                left[0] * xa[0:1] + left[1] * xa[1:2] + left[2] * xa[2:3], axis=1, keepdims=True
            )
            for c in range(3):
                far_terms[pl.ds(8 * f + c, 1), :] = jnp.sum(left[c] * coef_b, axis=0, keepdims=True)
                far_terms[pl.ds(8 * f + 4 + c, 1), :] = jnp.sum(
                    right[c] * coef_a, axis=0, keepdims=True
                )

        def step(h, carry):
            for u in range(4):
                one(4 * h + u)
            return carry

        lax.fori_loop(0, far // 4, step, 0)

    places = (
        ((0, 0),),
        ((0, 1), (1, 0)),
        ((0, 2), (2, 0)),
        ((1, 1),),
        ((1, 2), (2, 1)),
        ((2, 2),),
    )
    sub_id = lax.broadcasted_iota(i32, (8, lanes), 0)
    comp = sub_id % 4

    def spread_density(rows):
        split = []
        for i in range(3):
            row = rows[i : i + 1]
            high = row.astype(bf16).astype(f32)
            split.append(jnp.where(sub_id < 4, high, row - high))
        empty = jnp.zeros((8, lanes), f32)
        out = []
        for place in places:
            value = empty
            for r, i in place:
                value = jnp.where(comp == r, split[i], value)
            out.append(jnp.concatenate([value, empty], axis=0).astype(bf16))
        return out

    def near_pair(recv, p, block, at):
        owner_a, rank_a = entry_slot(0, p)
        owner_b, rank_b = entry_slot(0, near + p)
        weight_a = points[p, 3, 0:1, :]
        weight_b = points[p, 3, 4:5, :]
        a = spread_density(recv[owner_a, rank_a] * weight_a)
        b = spread_density(recv[owner_b, rank_b] * weight_b)
        into_b = jnp.zeros((8, lanes), f32)
        for q in range(6):
            into_b = into_b + jnp.dot(
                jnp.concatenate([a[q], a[q]], axis=1),
                block[at, :, pl.ds(q * lanes, lanes)],
                preferred_element_type=f32,
            )[0:8]
        back = lax.dot_general(
            jnp.concatenate(b, axis=1),
            block[at],
            (((1,), (1,)), ((), ())),
            preferred_element_type=f32,
        )
        into_a = back[0:8, :lanes] + back[0:8, lanes:]
        into_a = (into_a + pltpu.roll(into_a, 4, 0)) * weight_a
        into_b = (into_b + pltpu.roll(into_b, 4, 0)) * weight_b
        near_terms[pl.ds(pl.multiple_of(8 * p, 8), 8), :] = jnp.where(sub_id < 4, into_a, into_b)

    def apply_quarter(k, recv):
        def step(h, carry):
            for u in range(4):
                near_pair(recv, k * quarter + 4 * h + u, blocks[k], 4 * h + u)
            return carry

        lax.fori_loop(0, quarter // 4, step, 0)

    def fill_terms(send, source, row):
        def fill(o):
            for k in range(2):
                entry = jnp.clip(tab_s[row + k, o], 0, lanes)
                send[o, k] = source[pl.ds(4 * entry, 3), :]

        return fill

    def reduce_terms(stage, target, here):
        for c in range(3):
            total = jnp.zeros((clusters, lanes), f32)
            for k in range(2):
                total = total + jnp.dot(
                    one_hot[k, :, pl.ds(0, n)],
                    near_recv[stage, :, k, c, :],
                    precision=highest,
                    preferred_element_type=f32,
                )
                total = total + jnp.dot(
                    one_hot[2 + k, :, pl.ds(0, n)],
                    far_recv[stage, :, k, c, :],
                    precision=highest,
                    preferred_element_type=f32,
                )
            target[c] = total
            if here is not None:
                here[:, c, :] = total

    def mean_of(u, v):
        return jnp.sum(jnp.sum(u * v, axis=0), keepdims=True) * (1.0 / size_all)

    def send_sums(which, values):
        lane_row = lax.broadcasted_iota(i32, (1, lanes), 1)
        row = jnp.zeros((1, lanes), f32)
        for j, value in enumerate(values):
            row = jnp.where(lane_row == j, value, row)
        sum_send[which] = row
        pltpu.make_async_copy(
            sum_send.at[which], sum_recv.at[which, me], recv_sem.at[7 + which]
        ).start()

        def step(i, carry):
            peer = lax.rem(me + i, n)
            pltpu.make_async_remote_copy(
                sum_send.at[which],
                sum_recv.at[which, me],
                send_sem.at[7 + which],
                recv_sem.at[7 + which],
                device_id=(peer,),
                device_id_type=mesh_id,
            ).start()
            return carry

        lax.fori_loop(1, n, step, 0)

    def take_sums(which, count):
        arrived(sum_recv.at[which], 7 + which)
        total = jnp.sum(sum_recv[which], axis=0)
        return [total[0:1, j : j + 1] for j in range(count)]

    spread_first(0, cols_even)
    make_quarter(0, None)
    arrived(x_recv, 2)
    apply_far(x_recv, 2)
    exchange(far_send.at[0], far_recv.at[0], 3, fill_terms(far_send.at[0], far_terms, 4))
    for k in range(1, 4):
        make_quarter(k, x_recv)
    apply_quarter(3, x_recv)
    exchange(near_send.at[0], near_recv.at[0], 4, fill_terms(near_send.at[0], near_terms, 2))
    arrived(far_recv.at[0], 3)
    arrived(near_recv.at[0], 4)
    reduce_terms(0, y_all, y_here)

    exchange(yn_send, yn_recv, 9, fill_density(yn_send, y_here, (0, 1)))
    exchange(yf_send, yf_recv, 10, fill_density(yf_send, y_here, (2, 3)))
    x = x_ref[...]
    y = y_all[...]
    send_sums(0, [mean_of(x, x), mean_of(x, y), mean_of(y, y)])
    arrived(yn_recv, 9)
    apply_quarter(0, yn_recv)
    apply_quarter(1, yn_recv)
    arrived(yf_recv, 10)
    apply_far(yf_recv, 0)
    exchange(far_send.at[1], far_recv.at[1], 5, fill_terms(far_send.at[1], far_terms, 4))
    apply_quarter(2, yn_recv)
    apply_quarter(3, yn_recv)
    exchange(near_send.at[1], near_recv.at[1], 6, fill_terms(near_send.at[1], near_terms, 2))
    xx, xy, yy = take_sums(0, 3)
    scale_sq = xx + norm_eps
    scale = jnp.sqrt(scale_sq)
    proj_first = xy / scale_sq
    resid_sq = (yy - proj_first * xy * (1.0 + norm_eps / scale_sq)) / scale_sq
    norm_sq = resid_sq + norm_eps
    norm_first = jnp.sqrt(norm_sq)
    shrink = 1.0 / (scale * norm_first)
    x = x_ref[...]
    y = y_all[...]
    basis_one = x / scale
    basis_two = (y - proj_first * x) * shrink
    basis_ref[0] = basis_two
    arrived(far_recv.at[1], 5)
    arrived(near_recv.at[1], 6)
    reduce_terms(1, z_all, None)
    image_two = (z_all[...] - proj_first * y_all[...]) * shrink
    send_sums(
        1, [mean_of(basis_one, image_two), mean_of(basis_two, image_two), mean_of(image_two, image_two)]
    )
    cross, second, image_sq = take_sums(1, 3)
    one_sq = xx / scale_sq
    two_sq = resid_sq / norm_sq
    one_two = xy * norm_eps / (scale_sq * scale_sq * norm_first)
    last_sq = (
        image_sq
        + cross * cross * (one_sq - 2.0)
        + second * second * (two_sq - 2.0)
        + 2.0 * cross * second * one_two
    )
    norm_second = jnp.sqrt(last_sq + norm_eps)
    shrink_two = 1.0 / norm_second
    basis_ref[1] = (image_two - cross * basis_one - second * basis_two) * shrink_two
    row_id = lax.broadcasted_iota(i32, (2, 3), 1)
    col_id = lax.broadcasted_iota(i32, (2, 3), 0)
    hess = jnp.zeros((2, 3), f32)
    placed = (
        (0, 0, proj_first),
        (0, 1, cross),
        (1, 0, norm_first),
        (1, 1, second),
        (2, 1, norm_second),
    )
    for r, c, value in placed:
        hess = jnp.where((row_id == r) & (col_id == c), value, hess)
    hess_ref[...] = hess

    sent(req_send, 0)
    sent(geo_send, 1)
    sent(x_send, 2)
    sent(far_send.at[0], 3)
    sent(near_send.at[0], 4)
    sent(far_send.at[1], 5)
    sent(near_send.at[1], 6)
    sent(yn_send, 9)
    sent(yf_send, 10)
    for which in range(2):
        sent(sum_recv.at[which], 7 + which)


def per_device(
    right_side, vertices, panels, near_owner, near_local, far_owner, far_local, far_left, far_right
):
    n = lax.axis_size("dev")
    near = near_owner.shape[0]
    far = far_owner.shape[0]
    clusters = right_side.shape[0]

    vmem = pltpu.VMEM
    basis, hess = pl.pallas_call(
        functools.partial(kernel, n, near, far),
        out_shape=(
            jax.ShapeDtypeStruct((2, 3, clusters, lanes), f32),
            jax.ShapeDtypeStruct((2, 3), f32),
        ),
        in_specs=[pl.BlockSpec(memory_space=vmem)] * 9,
        out_specs=(pl.BlockSpec(memory_space=vmem),) * 2,
        scratch_shapes=[
            vmem((n, 1, lanes), f32),
            vmem((n, 1, lanes), f32),
            vmem((8, lanes), i32),
            pltpu.SMEM((8, lanes), i32),
            vmem((8, lanes), i32),
            pltpu.SMEM((8, lanes), i32),
            vmem((4, clusters, lanes), f32),
            vmem((clusters, 3, lanes), f32),
            vmem((clusters, 3, lanes), f32),
            vmem((clusters, 3, lanes), f32),
            vmem((n, 2, 2, 3, lanes), f32),
            vmem((n, 2, 2, 3, lanes), f32),
            vmem((n, 4, 3, lanes), f32),
            vmem((n, 4, 3, lanes), f32),
            vmem((n, 2, 3, lanes), f32),
            vmem((n, 2, 3, lanes), f32),
            vmem((n, 2, 3, lanes), f32),
            vmem((n, 2, 3, lanes), f32),
            vmem((2, n, 2, 3, lanes), f32),
            vmem((2, n, 2, 3, lanes), f32),
            vmem((2, n, 2, 3, lanes), f32),
            vmem((2, n, 2, 3, lanes), f32),
            vmem((near, 4, 8, lanes), f32),
            vmem((32 * near, lanes), f32),
            vmem((near // 4, lanes, lanes), bf16),
            vmem((4, lanes, 9 * lanes), bf16),
            vmem((lanes, 9 * lanes), f32),
            vmem((lanes, 9 * lanes), f32),
            vmem((near // 4, 2 * lanes, 6 * lanes), bf16),
            vmem((near // 4, 2 * lanes, 6 * lanes), bf16),
            vmem((near // 4, 2 * lanes, 6 * lanes), bf16),
            vmem((near // 4, 2 * lanes, 6 * lanes), bf16),
            vmem((4 * lanes + 8, lanes), f32),
            vmem((4 * lanes + 8, lanes), f32),
            vmem((3, clusters, lanes), f32),
            vmem((3, clusters, lanes), f32),
            vmem((clusters, 3, lanes), f32),
            vmem((2, 1, lanes), f32),
            vmem((2, n, 1, lanes), f32),
            pltpu.SemaphoreType.DMA((11,)),
            pltpu.SemaphoreType.DMA((11,)),
            pltpu.SemaphoreType.DMA((2,)),
        ],
        compiler_params=pltpu.CompilerParams(
            collective_id=0, has_side_effects=True, vmem_limit_bytes=58 * 1024 * 1024
        ),
    )(
        near_owner.T,
        near_local.T,
        far_owner.T,
        far_local.T,
        right_side.transpose(1, 0, 2),
        vertices.transpose(1, 0, 2),
        panels.transpose(1, 0, 2),
        far_left,
        far_right,
    )
    return basis.transpose(0, 2, 1, 3), hess.T


def solution(mesh):
    block = P("dev", None, None)
    pair = P("dev", None)
    return jax.shard_map(
        per_device,
        mesh=mesh,
        in_specs=(block, block, block, pair, pair, pair, pair, block, block),
        out_specs=(P(None, "dev", None, None), P()),
        check_vma=False,
    )
```

```python
import functools

import jax
import jax.numpy as jnp
from jax import lax
from jax.experimental import pallas as pl
from jax.experimental.pallas import tpu as pltpu
from jax.sharding import PartitionSpec as P

highest = lax.Precision.HIGHEST
soft_sq = 0.0025
area_floor = 6.25e-06
kelvin_diag = 1.8
norm_eps = 1e-06
lanes = 128
f32 = jnp.float32
i32 = jnp.int32
bf16 = jnp.bfloat16
mesh_id = pl.DeviceIdType.MESH


def list_tables(owners, locals_, count):
    owner_row = jnp.concatenate([owners[0:1], owners[1:2]], axis=1).astype(f32)
    local_row = jnp.concatenate([locals_[0:1], locals_[1:2]], axis=1).astype(f32)
    shape = (lanes, lanes)
    sub = lax.broadcasted_iota(i32, shape, 0)
    lane = lax.broadcasted_iota(i32, shape, 1)
    tile = (2 * (sub % count) + sub // count - lanes).astype(f32)
    lane_f = lane.astype(f32)
    owner_b = jnp.broadcast_to(owner_row, shape)
    owner_t = owner_b.T
    local_t = jnp.broadcast_to(local_row, shape).T
    same = owner_b == owner_t
    rank_row = jnp.sum(jnp.where(same & (sub < lane), 1.0, 0.0), axis=0, keepdims=True)
    rank_col = jnp.sum(jnp.where(same & (lane < sub), 1.0, 0.0), axis=1, keepdims=True)
    slot_row = owner_row * 2.0 + rank_row
    requests, entries = [], []
    for k in range(2):
        hit = (owner_t == lane_f) & (rank_col == float(k))
        requests.append(jnp.sum(jnp.where(hit, local_t, 0.0), axis=0, keepdims=True))
        entries.append(
            jnp.sum(jnp.where(hit, tile, 0.0), axis=0, keepdims=True) + float(lanes)
        )
    return slot_row, requests, entries


def three_parts(rows):
    high = rows.astype(bf16).astype(f32)
    rest = rows - high
    middle = rest.astype(bf16).astype(f32)
    return [high, middle, rest - middle]


def kernel(
    n,
    near,
    far,
    near_owner_ref,
    near_local_ref,
    far_owner_ref,
    far_local_ref,
    x_ref,
    vert_ref,
    panel_ref,
    left_ref,
    right_ref,
    basis_ref,
    hess_ref,
    req_send,
    req_recv,
    tab_v,
    tab_s,
    ask_v,
    ask_s,
    one_hot,
    x_here,
    vert_here,
    panel_here,
    geo_send,
    geo_recv,
    x_send,
    x_recv,
    yn_send,
    yn_recv,
    yf_send,
    yf_recv,
    near_send,
    near_recv,
    far_send,
    far_recv,
    points,
    first_rows,
    first_cols,
    picker,
    cols_even,
    cols_odd,
    blocks_0,
    blocks_1,
    blocks_2,
    blocks_3,
    near_terms,
    far_terms,
    y_all,
    z_all,
    y_here,
    sum_send,
    sum_recv,
    send_sem,
    recv_sem,
    local_sem,
):
    me = lax.axis_index("dev")
    clusters = x_ref.shape[1]
    blocks = (blocks_0, blocks_1, blocks_2, blocks_3)
    size_all = float(clusters * n * 3 * lanes)

    barrier = pltpu.get_barrier_semaphore()

    def every_peer(body):
        group = 4
        count = (n - 1) // group

        def step(g, carry):
            for u in range(group):
                body(lax.rem(me + (1 + group * g + u), n))
            return carry

        lax.fori_loop(0, count, step, 0)
        for i in range(1 + group * count, n):
            body(lax.rem(me + i, n))

    def greet(peer):
        pl.semaphore_signal(barrier, inc=1, device_id=(peer,), device_id_type=mesh_id)

    every_peer(greet)

    def asked_id(k, o):
        return jnp.clip(ask_s[k, o], 0, clusters - 1)

    def entry_slot(row, e):
        slot = jnp.clip(tab_s[row, e], 0, 2 * n - 1)
        return slot >> 1, slot & 1

    near_slot, near_req, near_entry = list_tables(near_owner_ref[...], near_local_ref[...], near)
    far_slot, far_req, far_entry = list_tables(far_owner_ref[...], far_local_ref[...], far)
    rows = [near_slot, far_slot] + near_entry + far_entry
    tab_v[...] = jnp.concatenate(rows + [jnp.zeros((2, lanes), f32)], axis=0).astype(i32)
    to_smem = pltpu.make_async_copy(tab_v, tab_s, local_sem.at[0])
    to_smem.start()
    req_rows = jnp.concatenate(near_req + far_req + [jnp.zeros((lanes - 4, lanes), f32)], axis=0)
    req_send[...] = req_rows.T[:n].reshape(n, 1, lanes)
    pl.semaphore_wait(barrier, n - 1)

    def exchange(send, recv, which, fill):
        fill(me)
        pltpu.make_async_copy(send.at[me], recv.at[me], recv_sem.at[which]).start()

        def step(peer):
            fill(peer)
            pltpu.make_async_remote_copy(
                send.at[peer],
                recv.at[me],
                send_sem.at[which],
                recv_sem.at[which],
                device_id=(peer,),
                device_id_type=mesh_id,
            ).start()

        every_peer(step)

    def arrived(recv, which):
        pltpu.make_async_copy(recv, recv, recv_sem.at[which]).wait()

    def sent(send, which):
        part = send.at[pl.ds(0, n - 1)]
        pltpu.make_async_copy(part, part, send_sem.at[which]).wait()

    exchange(req_send, req_recv, 0, lambda o: None)
    for c in range(3):
        x_here[:, c, :] = x_ref[c]
        vert_here[:, c, :] = vert_ref[c]
        panel_here[:, c, :] = panel_ref[c].astype(f32)
    near_terms[pl.ds(4 * lanes, 8), :] = jnp.zeros((8, lanes), f32)
    far_terms[pl.ds(4 * lanes, 8), :] = jnp.zeros((8, lanes), f32)

    picked = lax.broadcasted_iota(i32, (lanes, lanes), 0)
    for r in range(4):
        for j in range(9):
            place = picked - 32 * r
            if j < 8:
                hit = (place == j) | (place == 8 + j) | (place == 16 + j)
            else:
                hit = (place >= 24) & (place < 27)
            picker[r, :, pl.ds(j * lanes, lanes)] = jnp.where(hit, 1.0, 0.0).astype(bf16)

    arrived(req_recv, 0)
    asked = req_recv[...].reshape(n, lanes)
    if n < lanes:
        asked = jnp.concatenate([asked, jnp.zeros((lanes - n, lanes), f32)], axis=0)
    asked = asked.T
    ask_v[...] = asked[0:8].astype(i32)
    ask_copy = pltpu.make_async_copy(ask_v, ask_s, local_sem.at[1])
    ask_copy.start()
    cluster_ids = lax.broadcasted_iota(i32, (clusters, lanes), 0).astype(f32)
    for k in range(4):
        one_hot[k] = jnp.where(cluster_ids == asked[k : k + 1], 1.0, 0.0)
    ask_copy.wait()
    to_smem.wait()

    def fill_geo(o):
        for k in range(2):
            c = asked_id(k, o)
            geo_send[o, k, 0] = vert_here[c]
            geo_send[o, k, 1] = panel_here[c]

    def fill_density(send, source, slots):
        def fill(o):
            for j, k in enumerate(slots):
                send[o, j] = source[asked_id(k, o)]

        return fill

    exchange(geo_send, geo_recv, 1, fill_geo)
    exchange(x_send, x_recv, 2, fill_density(x_send, x_here, (0, 1, 2, 3)))
    arrived(geo_recv, 1)

    def make_points(p):
        owner_a, rank_a = entry_slot(0, p)
        owner_b, rank_b = entry_slot(0, near + p)
        va = geo_recv[owner_a, rank_a, 0]
        vb = geo_recv[owner_b, rank_b, 0]
        pa = geo_recv[owner_a, rank_a, 1].astype(i32)
        pb = geo_recv[owner_b, rank_b, 1].astype(i32)
        table = jnp.concatenate([va, va[0:1], vb, vb[0:1]], axis=0)
        corners = []
        for m in range(3):
            picks = jnp.concatenate(
                [
                    jnp.broadcast_to(pa[m : m + 1], (4, lanes)),
                    jnp.broadcast_to(pb[m : m + 1], (4, lanes)),
                ],
                axis=0,
            )
            corners.append(
                jnp.take_along_axis(table, picks, axis=1, mode="promise_in_bounds")
            )
        edge_one = corners[1] - corners[0]
        edge_two = corners[2] - corners[0]
        cross = edge_one * pltpu.roll(edge_two, 7, 0) - pltpu.roll(edge_one, 7, 0) * edge_two
        squares = cross * cross
        area = squares + pltpu.roll(squares, 7, 0) + pltpu.roll(squares, 6, 0)
        weight = jnp.sqrt(area + area_floor) / 6.0
        for s in range(3):
            others = [corners[m] for m in range(3) if m != s]
            points[p, s] = (2.0 / 3.0) * corners[s] + (1.0 / 6.0) * (others[0] + others[1])
        points[p, 3] = weight
        firsts = [points[p, s] for s in range(3)]
        head = jnp.concatenate([firsts[0][0:3], firsts[1][0:3], firsts[2][0:2]], axis=0)
        head_parts, tail_parts = three_parts(head), three_parts(firsts[2])
        first_rows[pl.ds(pl.multiple_of(32 * p, 32), 32), :] = jnp.concatenate(
            head_parts + [part[2:3] for part in tail_parts] + [jnp.zeros((5, lanes), f32)], axis=0
        )

    def points_step(h, carry):
        for u in range(4):
            make_points(4 * h + u)
        return carry

    lax.fori_loop(0, near // 4, points_step, 0)

    def turn_points(g, carry):
        rows = first_rows[pl.ds(pl.multiple_of(lanes * g, lanes), lanes), :]
        first_cols[g] = rows.T.astype(bf16)
        return carry

    lax.fori_loop(0, near // 4, turn_points, 0)

    chunk = 16

    def spread_first(p, target):
        target[...] = jnp.dot(first_cols[p // 4], picker[p % 4], preferred_element_type=f32)

    def make_block(p, cols, target, at):
        for c in range(lanes // chunk):
            at_rows = pl.ds(c * chunk, chunk)
            inv_sum = jnp.zeros((chunk, lanes), f32)
            cube_sum = jnp.zeros((chunk, lanes), f32)
            outer = [jnp.zeros((chunk, lanes), f32) for _ in range(5)]
            for s in range(3):
                a = [cols[at_rows, pl.ds((3 * s + i) * lanes, lanes)] for i in range(3)]
                for t in range(3):
                    d = [a[i] - points[p, t, 4 + i : 5 + i, :] for i in range(3)]
                    inv = lax.rsqrt(d[0] * d[0] + d[1] * d[1] + (d[2] * d[2] + soft_sq))
                    cube = inv * inv * inv
                    e0 = cube * d[0]
                    e1 = cube * d[1]
                    inv_sum = inv_sum + inv
                    cube_sum = cube_sum + cube
                    outer = [
                        outer[0] + e0 * d[0],
                        outer[1] + e0 * d[1],
                        outer[2] + e0 * d[2],
                        outer[3] + e1 * d[1],
                        outer[4] + e1 * d[2],
                    ]
            last = inv_sum - soft_sq * cube_sum - outer[0] - outer[3]
            diag = kelvin_diag * inv_sum
            entries = (
                outer[0] + diag,
                outer[1],
                outer[2],
                outer[3] + diag,
                outer[4],
                last + diag,
            )
            for q in range(6):
                value = entries[q]
                high = value.astype(bf16)
                at_lanes = pl.ds(q * lanes, lanes)
                target[at, at_rows, at_lanes] = high
                target[at, pl.ds(lanes + c * chunk, chunk), at_lanes] = (
                    value - high.astype(f32)
                ).astype(bf16)

    quarter = near // 4

    def make_quarter(k, recv):
        def step(h, carry):
            at = 2 * h
            p = k * quarter + at
            spread_first(p + 1, cols_odd)
            if recv is not None:
                near_pair(recv, p - quarter, blocks[k - 1], at)
            make_block(p, cols_even, blocks[k], at)
            spread_first(jnp.minimum(p + 2, near - 1), cols_even)
            if recv is not None:
                near_pair(recv, p + 1 - quarter, blocks[k - 1], at + 1)
            make_block(p + 1, cols_odd, blocks[k], at + 1)
            return carry

        lax.fori_loop(0, quarter // 2, step, 0)

    def apply_far(recv, base):
        def one(f):
            owner_a, rank_a = entry_slot(1, f)
            owner_b, rank_b = entry_slot(1, far + f)
            xa = recv[owner_a, base + rank_a]
            xb = recv[owner_b, base + rank_b]
            left = [left_ref[f, :, pl.ds(c * lanes, lanes)] for c in range(3)]
            right = [right_ref[f, :, pl.ds(c * lanes, lanes)] for c in range(3)]
            coef_b = jnp.sum(
                right[0] * xb[0:1] + right[1] * xb[1:2] + right[2] * xb[2:3], axis=1, keepdims=True
            )
            coef_a = jnp.sum(
                left[0] * xa[0:1] + left[1] * xa[1:2] + left[2] * xa[2:3], axis=1, keepdims=True
            )
            for c in range(3):
                far_terms[pl.ds(8 * f + c, 1), :] = jnp.sum(left[c] * coef_b, axis=0, keepdims=True)
                far_terms[pl.ds(8 * f + 4 + c, 1), :] = jnp.sum(
                    right[c] * coef_a, axis=0, keepdims=True
                )

        def step(h, carry):
            for u in range(4):
                one(4 * h + u)
            return carry

        lax.fori_loop(0, far // 4, step, 0)

    places = (
        ((0, 0),),
        ((0, 1), (1, 0)),
        ((0, 2), (2, 0)),
        ((1, 1),),
        ((1, 2), (2, 1)),
        ((2, 2),),
    )
    sub_id = lax.broadcasted_iota(i32, (8, lanes), 0)
    comp = sub_id % 4

    def spread_density(rows):
        split = []
        for i in range(3):
            row = rows[i : i + 1]
            high = row.astype(bf16).astype(f32)
            split.append(jnp.where(sub_id < 4, high, row - high))
        empty = jnp.zeros((8, lanes), f32)
        out = []
        for place in places:
            value = empty
            for r, i in place:
                value = jnp.where(comp == r, split[i], value)
            out.append(jnp.concatenate([value, empty], axis=0).astype(bf16))
        return out

    def near_pair(recv, p, block, at):
        owner_a, rank_a = entry_slot(0, p)
        owner_b, rank_b = entry_slot(0, near + p)
        weight_a = points[p, 3, 0:1, :]
        weight_b = points[p, 3, 4:5, :]
        a = spread_density(recv[owner_a, rank_a] * weight_a)
        b = spread_density(recv[owner_b, rank_b] * weight_b)
        into_b = jnp.zeros((8, lanes), f32)
        for q in range(6):
            into_b = into_b + jnp.dot(
                jnp.concatenate([a[q], a[q]], axis=1),
                block[at, :, pl.ds(q * lanes, lanes)],
                preferred_element_type=f32,
            )[0:8]
        back = lax.dot_general(
            jnp.concatenate(b, axis=1),
            block[at],
            (((1,), (1,)), ((), ())),
            preferred_element_type=f32,
        )
        into_a = back[0:8, :lanes] + back[0:8, lanes:]
        into_a = (into_a + pltpu.roll(into_a, 4, 0)) * weight_a
        into_b = (into_b + pltpu.roll(into_b, 4, 0)) * weight_b
        near_terms[pl.ds(pl.multiple_of(8 * p, 8), 8), :] = jnp.where(sub_id < 4, into_a, into_b)

    def apply_quarter(k, recv):
        def step(h, carry):
            for u in range(4):
                near_pair(recv, k * quarter + 4 * h + u, blocks[k], 4 * h + u)
            return carry

        lax.fori_loop(0, quarter // 4, step, 0)

    def fill_terms(send, source, row):
        def fill(o):
            for k in range(2):
                entry = jnp.clip(tab_s[row + k, o], 0, lanes)
                send[o, k] = source[pl.ds(4 * entry, 3), :]

        return fill

    def reduce_terms(stage, target, here):
        for c in range(3):
            total = jnp.zeros((clusters, lanes), f32)
            for k in range(2):
                total = total + jnp.dot(
                    one_hot[k, :, pl.ds(0, n)],
                    near_recv[stage, :, k, c, :],
                    precision=highest,
                    preferred_element_type=f32,
                )
                total = total + jnp.dot(
                    one_hot[2 + k, :, pl.ds(0, n)],
                    far_recv[stage, :, k, c, :],
                    precision=highest,
                    preferred_element_type=f32,
                )
            target[c] = total
            if here is not None:
                here[:, c, :] = total

    def mean_of(u, v):
        return jnp.sum(jnp.sum(u * v, axis=0), keepdims=True) * (1.0 / size_all)

    def send_sums(which, values):
        lane_row = lax.broadcasted_iota(i32, (1, lanes), 1)
        row = jnp.zeros((1, lanes), f32)
        for j, value in enumerate(values):
            row = jnp.where(lane_row == j, value, row)
        sum_send[which] = row
        pltpu.make_async_copy(
            sum_send.at[which], sum_recv.at[which, me], recv_sem.at[7 + which]
        ).start()

        def step(peer):
            pltpu.make_async_remote_copy(
                sum_send.at[which],
                sum_recv.at[which, me],
                send_sem.at[7 + which],
                recv_sem.at[7 + which],
                device_id=(peer,),
                device_id_type=mesh_id,
            ).start()

        every_peer(step)

    def take_sums(which, count):
        arrived(sum_recv.at[which], 7 + which)
        total = jnp.sum(sum_recv[which], axis=0)
        return [total[0:1, j : j + 1] for j in range(count)]

    spread_first(0, cols_even)
    make_quarter(0, None)
    arrived(x_recv, 2)
    apply_far(x_recv, 2)
    exchange(far_send.at[0], far_recv.at[0], 3, fill_terms(far_send.at[0], far_terms, 4))
    for k in range(1, 4):
        make_quarter(k, x_recv)
    apply_quarter(3, x_recv)
    exchange(near_send.at[0], near_recv.at[0], 4, fill_terms(near_send.at[0], near_terms, 2))
    arrived(far_recv.at[0], 3)
    arrived(near_recv.at[0], 4)
    reduce_terms(0, y_all, y_here)

    exchange(yn_send, yn_recv, 9, fill_density(yn_send, y_here, (0, 1)))
    exchange(yf_send, yf_recv, 10, fill_density(yf_send, y_here, (2, 3)))
    x = x_ref[...]
    y = y_all[...]
    send_sums(0, [mean_of(x, x), mean_of(x, y), mean_of(y, y)])
    arrived(yn_recv, 9)
    apply_quarter(0, yn_recv)
    apply_quarter(1, yn_recv)
    arrived(yf_recv, 10)
    apply_far(yf_recv, 0)
    exchange(far_send.at[1], far_recv.at[1], 5, fill_terms(far_send.at[1], far_terms, 4))
    apply_quarter(2, yn_recv)
    apply_quarter(3, yn_recv)
    exchange(near_send.at[1], near_recv.at[1], 6, fill_terms(near_send.at[1], near_terms, 2))
    xx, xy, yy = take_sums(0, 3)
    scale_sq = xx + norm_eps
    scale = jnp.sqrt(scale_sq)
    proj_first = xy / scale_sq
    resid_sq = (yy - proj_first * xy * (1.0 + norm_eps / scale_sq)) / scale_sq
    norm_sq = resid_sq + norm_eps
    norm_first = jnp.sqrt(norm_sq)
    shrink = 1.0 / (scale * norm_first)
    x = x_ref[...]
    y = y_all[...]
    basis_one = x / scale
    basis_two = (y - proj_first * x) * shrink
    basis_ref[0] = basis_two
    arrived(far_recv.at[1], 5)
    arrived(near_recv.at[1], 6)
    reduce_terms(1, z_all, None)
    image_two = (z_all[...] - proj_first * y_all[...]) * shrink
    send_sums(
        1, [mean_of(basis_one, image_two), mean_of(basis_two, image_two), mean_of(image_two, image_two)]
    )
    cross, second, image_sq = take_sums(1, 3)
    one_sq = xx / scale_sq
    two_sq = resid_sq / norm_sq
    one_two = xy * norm_eps / (scale_sq * scale_sq * norm_first)
    last_sq = (
        image_sq
        + cross * cross * (one_sq - 2.0)
        + second * second * (two_sq - 2.0)
        + 2.0 * cross * second * one_two
    )
    norm_second = jnp.sqrt(last_sq + norm_eps)
    shrink_two = 1.0 / norm_second
    basis_ref[1] = (image_two - cross * basis_one - second * basis_two) * shrink_two
    row_id = lax.broadcasted_iota(i32, (2, 3), 1)
    col_id = lax.broadcasted_iota(i32, (2, 3), 0)
    hess = jnp.zeros((2, 3), f32)
    placed = (
        (0, 0, proj_first),
        (0, 1, cross),
        (1, 0, norm_first),
        (1, 1, second),
        (2, 1, norm_second),
    )
    for r, c, value in placed:
        hess = jnp.where((row_id == r) & (col_id == c), value, hess)
    hess_ref[...] = hess

    sent(req_send, 0)
    sent(geo_send, 1)
    sent(x_send, 2)
    sent(far_send.at[0], 3)
    sent(near_send.at[0], 4)
    sent(far_send.at[1], 5)
    sent(near_send.at[1], 6)
    sent(yn_send, 9)
    sent(yf_send, 10)
    for which in range(2):
        sent(sum_recv.at[which], 7 + which)


def per_device(
    right_side, vertices, panels, near_owner, near_local, far_owner, far_local, far_left, far_right
):
    n = lax.axis_size("dev")
    near = near_owner.shape[0]
    far = far_owner.shape[0]
    clusters = right_side.shape[0]

    vmem = pltpu.VMEM
    basis, hess = pl.pallas_call(
        functools.partial(kernel, n, near, far),
        out_shape=(
            jax.ShapeDtypeStruct((2, 3, clusters, lanes), f32),
            jax.ShapeDtypeStruct((2, 3), f32),
        ),
        in_specs=[pl.BlockSpec(memory_space=vmem)] * 9,
        out_specs=(pl.BlockSpec(memory_space=vmem),) * 2,
        scratch_shapes=[
            vmem((n, 1, lanes), f32),
            vmem((n, 1, lanes), f32),
            vmem((8, lanes), i32),
            pltpu.SMEM((8, lanes), i32),
            vmem((8, lanes), i32),
            pltpu.SMEM((8, lanes), i32),
            vmem((4, clusters, lanes), f32),
            vmem((clusters, 3, lanes), f32),
            vmem((clusters, 3, lanes), f32),
            vmem((clusters, 3, lanes), f32),
            vmem((n, 2, 2, 3, lanes), f32),
            vmem((n, 2, 2, 3, lanes), f32),
            vmem((n, 4, 3, lanes), f32),
            vmem((n, 4, 3, lanes), f32),
            vmem((n, 2, 3, lanes), f32),
            vmem((n, 2, 3, lanes), f32),
            vmem((n, 2, 3, lanes), f32),
            vmem((n, 2, 3, lanes), f32),
            vmem((2, n, 2, 3, lanes), f32),
            vmem((2, n, 2, 3, lanes), f32),
            vmem((2, n, 2, 3, lanes), f32),
            vmem((2, n, 2, 3, lanes), f32),
            vmem((near, 4, 8, lanes), f32),
            vmem((32 * near, lanes), f32),
            vmem((near // 4, lanes, lanes), bf16),
            vmem((4, lanes, 9 * lanes), bf16),
            vmem((lanes, 9 * lanes), f32),
            vmem((lanes, 9 * lanes), f32),
            vmem((near // 4, 2 * lanes, 6 * lanes), bf16),
            vmem((near // 4, 2 * lanes, 6 * lanes), bf16),
            vmem((near // 4, 2 * lanes, 6 * lanes), bf16),
            vmem((near // 4, 2 * lanes, 6 * lanes), bf16),
            vmem((4 * lanes + 8, lanes), f32),
            vmem((4 * lanes + 8, lanes), f32),
            vmem((3, clusters, lanes), f32),
            vmem((3, clusters, lanes), f32),
            vmem((clusters, 3, lanes), f32),
            vmem((2, 1, lanes), f32),
            vmem((2, n, 1, lanes), f32),
            pltpu.SemaphoreType.DMA((11,)),
            pltpu.SemaphoreType.DMA((11,)),
            pltpu.SemaphoreType.DMA((4,)),
        ],
        compiler_params=pltpu.CompilerParams(
            collective_id=0, has_side_effects=True, vmem_limit_bytes=58 * 1024 * 1024
        ),
    )(
        near_owner.T,
        near_local.T,
        far_owner.T,
        far_local.T,
        right_side.transpose(1, 0, 2),
        vertices.transpose(1, 0, 2),
        panels.transpose(1, 0, 2),
        far_left,
        far_right,
    )
    return basis.transpose(0, 2, 1, 3), hess.T


def solution(mesh):
    block = P("dev", None, None)
    pair = P("dev", None)
    return jax.shard_map(
        per_device,
        mesh=mesh,
        in_specs=(block, block, block, pair, pair, pair, pair, block, block),
        out_specs=(P(None, "dev", None, None), P()),
        check_vma=False,
    )
```

```python
import functools

import jax
import jax.numpy as jnp
from jax import lax
from jax.experimental import pallas as pl
from jax.experimental.pallas import tpu as pltpu
from jax.sharding import PartitionSpec as P

highest = lax.Precision.HIGHEST
soft_sq = 0.0025
area_floor = 6.25e-06
kelvin_diag = 1.8
norm_eps = 1e-06
lanes = 128
f32 = jnp.float32
i32 = jnp.int32
bf16 = jnp.bfloat16
mesh_id = pl.DeviceIdType.MESH


def list_tables(owners, locals_, count):
    owner_row = jnp.concatenate([owners[0:1], owners[1:2]], axis=1).astype(f32)
    local_row = jnp.concatenate([locals_[0:1], locals_[1:2]], axis=1).astype(f32)
    shape = (lanes, lanes)
    sub = lax.broadcasted_iota(i32, shape, 0)
    lane = lax.broadcasted_iota(i32, shape, 1)
    tile = (2 * (sub % count) + sub // count - lanes).astype(f32)
    lane_f = lane.astype(f32)
    owner_b = jnp.broadcast_to(owner_row, shape)
    owner_t = owner_b.T
    local_t = jnp.broadcast_to(local_row, shape).T
    same = owner_b == owner_t
    rank_row = jnp.sum(jnp.where(same & (sub < lane), 1.0, 0.0), axis=0, keepdims=True)
    rank_col = jnp.sum(jnp.where(same & (lane < sub), 1.0, 0.0), axis=1, keepdims=True)
    slot_row = owner_row * 2.0 + rank_row
    requests, entries = [], []
    for k in range(2):
        hit = (owner_t == lane_f) & (rank_col == float(k))
        requests.append(jnp.sum(jnp.where(hit, local_t, 0.0), axis=0, keepdims=True))
        entries.append(
            jnp.sum(jnp.where(hit, tile, 0.0), axis=0, keepdims=True) + float(lanes)
        )
    return slot_row, requests, entries


def three_parts(rows):
    high = rows.astype(bf16).astype(f32)
    rest = rows - high
    middle = rest.astype(bf16).astype(f32)
    return [high, middle, rest - middle]


def kernel(
    n,
    near,
    far,
    near_owner_ref,
    near_local_ref,
    far_owner_ref,
    far_local_ref,
    x_ref,
    vert_ref,
    panel_ref,
    left_ref,
    right_ref,
    basis_ref,
    hess_ref,
    req_send,
    req_recv,
    tab_v,
    tab_s,
    ask_v,
    ask_s,
    one_hot,
    x_here,
    vert_here,
    panel_here,
    geo_send,
    geo_recv,
    x_send,
    x_recv,
    yn_send,
    yn_recv,
    yf_send,
    yf_recv,
    near_send,
    near_recv,
    far_send,
    far_recv,
    points,
    first_rows,
    first_cols,
    picker,
    cols_even,
    cols_odd,
    blocks_0,
    blocks_1,
    blocks_2,
    blocks_3,
    near_terms,
    far_terms,
    y_all,
    z_all,
    y_here,
    sum_send,
    sum_recv,
    inner_recv,
    outer_recv,
    send_sem,
    recv_sem,
    local_sem,
):
    me = lax.axis_index("dev")
    clusters = x_ref.shape[1]
    blocks = (blocks_0, blocks_1, blocks_2, blocks_3)
    size_all = float(clusters * n * 3 * lanes)

    barrier = pltpu.get_barrier_semaphore()

    def every_peer(body):
        group = 4
        count = (n - 1) // group

        def step(g, carry):
            for u in range(group):
                body(lax.rem(me + (1 + group * g + u), n))
            return carry

        lax.fori_loop(0, count, step, 0)
        for i in range(1 + group * count, n):
            body(lax.rem(me + i, n))

    def greet(peer):
        pl.semaphore_signal(barrier, inc=1, device_id=(peer,), device_id_type=mesh_id)

    every_peer(greet)

    def asked_id(k, o):
        return jnp.clip(ask_s[k, o], 0, clusters - 1)

    def entry_slot(row, e):
        slot = jnp.clip(tab_s[row, e], 0, 2 * n - 1)
        return slot >> 1, slot & 1

    near_slot, near_req, near_entry = list_tables(near_owner_ref[...], near_local_ref[...], near)
    far_slot, far_req, far_entry = list_tables(far_owner_ref[...], far_local_ref[...], far)
    rows = [near_slot, far_slot] + near_entry + far_entry
    tab_v[...] = jnp.concatenate(rows + [jnp.zeros((2, lanes), f32)], axis=0).astype(i32)
    to_smem = pltpu.make_async_copy(tab_v, tab_s, local_sem.at[0])
    to_smem.start()
    req_rows = jnp.concatenate(near_req + far_req + [jnp.zeros((lanes - 4, lanes), f32)], axis=0)
    req_send[...] = req_rows.T[:n].reshape(n, 1, lanes)
    pl.semaphore_wait(barrier, n - 1)

    def exchange(send, recv, which, fill):
        fill(me)
        pltpu.make_async_copy(send.at[me], recv.at[me], recv_sem.at[which]).start()

        def step(peer):
            fill(peer)
            pltpu.make_async_remote_copy(
                send.at[peer],
                recv.at[me],
                send_sem.at[which],
                recv_sem.at[which],
                device_id=(peer,),
                device_id_type=mesh_id,
            ).start()

        every_peer(step)

    def arrived(recv, which):
        pltpu.make_async_copy(recv, recv, recv_sem.at[which]).wait()

    def sent(send, which, count=n):
        part = send.at[pl.ds(0, count - 1)]
        pltpu.make_async_copy(part, part, send_sem.at[which]).wait()

    exchange(req_send, req_recv, 0, lambda o: None)
    for c in range(3):
        x_here[:, c, :] = x_ref[c]
        vert_here[:, c, :] = vert_ref[c]
        panel_here[:, c, :] = panel_ref[c].astype(f32)
    near_terms[pl.ds(4 * lanes, 8), :] = jnp.zeros((8, lanes), f32)
    far_terms[pl.ds(4 * lanes, 8), :] = jnp.zeros((8, lanes), f32)

    picked = lax.broadcasted_iota(i32, (lanes, lanes), 0)
    for r in range(4):
        for j in range(9):
            place = picked - 32 * r
            if j < 8:
                hit = (place == j) | (place == 8 + j) | (place == 16 + j)
            else:
                hit = (place >= 24) & (place < 27)
            picker[r, :, pl.ds(j * lanes, lanes)] = jnp.where(hit, 1.0, 0.0).astype(bf16)

    arrived(req_recv, 0)
    asked = req_recv[...].reshape(n, lanes)
    if n < lanes:
        asked = jnp.concatenate([asked, jnp.zeros((lanes - n, lanes), f32)], axis=0)
    asked = asked.T
    ask_v[...] = asked[0:8].astype(i32)
    ask_copy = pltpu.make_async_copy(ask_v, ask_s, local_sem.at[1])
    ask_copy.start()
    cluster_ids = lax.broadcasted_iota(i32, (clusters, lanes), 0).astype(f32)
    for k in range(4):
        one_hot[k] = jnp.where(cluster_ids == asked[k : k + 1], 1.0, 0.0)
    ask_copy.wait()
    to_smem.wait()

    def fill_geo(o):
        for k in range(2):
            c = asked_id(k, o)
            geo_send[o, k, 0] = vert_here[c]
            geo_send[o, k, 1] = panel_here[c]

    def fill_density(send, source, slots):
        def fill(o):
            for j, k in enumerate(slots):
                send[o, j] = source[asked_id(k, o)]

        return fill

    exchange(geo_send, geo_recv, 1, fill_geo)
    exchange(x_send, x_recv, 2, fill_density(x_send, x_here, (0, 1, 2, 3)))
    arrived(geo_recv, 1)

    def make_points(p):
        owner_a, rank_a = entry_slot(0, p)
        owner_b, rank_b = entry_slot(0, near + p)
        va = geo_recv[owner_a, rank_a, 0]
        vb = geo_recv[owner_b, rank_b, 0]
        pa = geo_recv[owner_a, rank_a, 1].astype(i32)
        pb = geo_recv[owner_b, rank_b, 1].astype(i32)
        table = jnp.concatenate([va, va[0:1], vb, vb[0:1]], axis=0)
        corners = []
        for m in range(3):
            picks = jnp.concatenate(
                [
                    jnp.broadcast_to(pa[m : m + 1], (4, lanes)),
                    jnp.broadcast_to(pb[m : m + 1], (4, lanes)),
                ],
                axis=0,
            )
            corners.append(
                jnp.take_along_axis(table, picks, axis=1, mode="promise_in_bounds")
            )
        edge_one = corners[1] - corners[0]
        edge_two = corners[2] - corners[0]
        cross = edge_one * pltpu.roll(edge_two, 7, 0) - pltpu.roll(edge_one, 7, 0) * edge_two
        squares = cross * cross
        area = squares + pltpu.roll(squares, 7, 0) + pltpu.roll(squares, 6, 0)
        weight = jnp.sqrt(area + area_floor) / 6.0
        for s in range(3):
            others = [corners[m] for m in range(3) if m != s]
            points[p, s] = (2.0 / 3.0) * corners[s] + (1.0 / 6.0) * (others[0] + others[1])
        points[p, 3] = weight
        firsts = [points[p, s] for s in range(3)]
        head = jnp.concatenate([firsts[0][0:3], firsts[1][0:3], firsts[2][0:2]], axis=0)
        head_parts, tail_parts = three_parts(head), three_parts(firsts[2])
        first_rows[pl.ds(pl.multiple_of(32 * p, 32), 32), :] = jnp.concatenate(
            head_parts + [part[2:3] for part in tail_parts] + [jnp.zeros((5, lanes), f32)], axis=0
        )

    def points_step(h, carry):
        for u in range(4):
            make_points(4 * h + u)
        return carry

    lax.fori_loop(0, near // 4, points_step, 0)

    def turn_points(g, carry):
        rows = first_rows[pl.ds(pl.multiple_of(lanes * g, lanes), lanes), :]
        first_cols[g] = rows.T.astype(bf16)
        return carry

    lax.fori_loop(0, near // 4, turn_points, 0)

    chunk = 16

    def spread_first(p, target):
        target[...] = jnp.dot(first_cols[p // 4], picker[p % 4], preferred_element_type=f32)

    def make_block(p, cols, target, at):
        for c in range(lanes // chunk):
            at_rows = pl.ds(c * chunk, chunk)
            inv_sum = jnp.zeros((chunk, lanes), f32)
            cube_sum = jnp.zeros((chunk, lanes), f32)
            outer = [jnp.zeros((chunk, lanes), f32) for _ in range(5)]
            for s in range(3):
                a = [cols[at_rows, pl.ds((3 * s + i) * lanes, lanes)] for i in range(3)]
                for t in range(3):
                    d = [a[i] - points[p, t, 4 + i : 5 + i, :] for i in range(3)]
                    inv = lax.rsqrt(d[0] * d[0] + d[1] * d[1] + (d[2] * d[2] + soft_sq))
                    cube = inv * inv * inv
                    e0 = cube * d[0]
                    e1 = cube * d[1]
                    inv_sum = inv_sum + inv
                    cube_sum = cube_sum + cube
                    outer = [
                        outer[0] + e0 * d[0],
                        outer[1] + e0 * d[1],
                        outer[2] + e0 * d[2],
                        outer[3] + e1 * d[1],
                        outer[4] + e1 * d[2],
                    ]
            last = inv_sum - soft_sq * cube_sum - outer[0] - outer[3]
            diag = kelvin_diag * inv_sum
            entries = (
                outer[0] + diag,
                outer[1],
                outer[2],
                outer[3] + diag,
                outer[4],
                last + diag,
            )
            for q in range(6):
                value = entries[q]
                high = value.astype(bf16)
                at_lanes = pl.ds(q * lanes, lanes)
                target[at, at_rows, at_lanes] = high
                target[at, pl.ds(lanes + c * chunk, chunk), at_lanes] = (
                    value - high.astype(f32)
                ).astype(bf16)

    quarter = near // 4

    def make_quarter(k, recv):
        def step(h, carry):
            at = 2 * h
            p = k * quarter + at
            spread_first(p + 1, cols_odd)
            if recv is not None:
                near_pair(recv, p - quarter, blocks[k - 1], at)
            make_block(p, cols_even, blocks[k], at)
            spread_first(jnp.minimum(p + 2, near - 1), cols_even)
            if recv is not None:
                near_pair(recv, p + 1 - quarter, blocks[k - 1], at + 1)
            make_block(p + 1, cols_odd, blocks[k], at + 1)
            return carry

        lax.fori_loop(0, quarter // 2, step, 0)

    def apply_far(recv, base):
        def one(f):
            owner_a, rank_a = entry_slot(1, f)
            owner_b, rank_b = entry_slot(1, far + f)
            xa = recv[owner_a, base + rank_a]
            xb = recv[owner_b, base + rank_b]
            left = [left_ref[f, :, pl.ds(c * lanes, lanes)] for c in range(3)]
            right = [right_ref[f, :, pl.ds(c * lanes, lanes)] for c in range(3)]
            coef_b = jnp.sum(
                right[0] * xb[0:1] + right[1] * xb[1:2] + right[2] * xb[2:3], axis=1, keepdims=True
            )
            coef_a = jnp.sum(
                left[0] * xa[0:1] + left[1] * xa[1:2] + left[2] * xa[2:3], axis=1, keepdims=True
            )
            for c in range(3):
                far_terms[pl.ds(8 * f + c, 1), :] = jnp.sum(left[c] * coef_b, axis=0, keepdims=True)
                far_terms[pl.ds(8 * f + 4 + c, 1), :] = jnp.sum(
                    right[c] * coef_a, axis=0, keepdims=True
                )

        def step(h, carry):
            for u in range(4):
                one(4 * h + u)
            return carry

        lax.fori_loop(0, far // 4, step, 0)

    places = (
        ((0, 0),),
        ((0, 1), (1, 0)),
        ((0, 2), (2, 0)),
        ((1, 1),),
        ((1, 2), (2, 1)),
        ((2, 2),),
    )
    sub_id = lax.broadcasted_iota(i32, (8, lanes), 0)
    comp = sub_id % 4

    def spread_density(rows):
        split = []
        for i in range(3):
            row = rows[i : i + 1]
            high = row.astype(bf16).astype(f32)
            split.append(jnp.where(sub_id < 4, high, row - high))
        empty = jnp.zeros((8, lanes), f32)
        out = []
        for place in places:
            value = empty
            for r, i in place:
                value = jnp.where(comp == r, split[i], value)
            out.append(jnp.concatenate([value, empty], axis=0).astype(bf16))
        return out

    def near_pair(recv, p, block, at):
        owner_a, rank_a = entry_slot(0, p)
        owner_b, rank_b = entry_slot(0, near + p)
        weight_a = points[p, 3, 0:1, :]
        weight_b = points[p, 3, 4:5, :]
        a = spread_density(recv[owner_a, rank_a] * weight_a)
        b = spread_density(recv[owner_b, rank_b] * weight_b)
        into_b = jnp.zeros((8, lanes), f32)
        for q in range(6):
            into_b = into_b + jnp.dot(
                jnp.concatenate([a[q], a[q]], axis=1),
                block[at, :, pl.ds(q * lanes, lanes)],
                preferred_element_type=f32,
            )[0:8]
        back = lax.dot_general(
            jnp.concatenate(b, axis=1),
            block[at],
            (((1,), (1,)), ((), ())),
            preferred_element_type=f32,
        )
        into_a = back[0:8, :lanes] + back[0:8, lanes:]
        into_a = (into_a + pltpu.roll(into_a, 4, 0)) * weight_a
        into_b = (into_b + pltpu.roll(into_b, 4, 0)) * weight_b
        near_terms[pl.ds(pl.multiple_of(8 * p, 8), 8), :] = jnp.where(sub_id < 4, into_a, into_b)

    def apply_quarter(k, recv):
        def step(h, carry):
            for u in range(4):
                near_pair(recv, k * quarter + 4 * h + u, blocks[k], 4 * h + u)
            return carry

        lax.fori_loop(0, quarter // 4, step, 0)

    def fill_terms(send, source, row):
        def fill(o):
            for k in range(2):
                entry = jnp.clip(tab_s[row + k, o], 0, lanes)
                send[o, k] = source[pl.ds(4 * entry, 3), :]

        return fill

    def gathered(recv, stage, first, c):
        total = jnp.zeros((clusters, lanes), f32)
        for k in range(2):
            total = total + jnp.dot(
                one_hot[first + k, :, pl.ds(0, n)],
                recv[stage, :, k, c, :],
                precision=highest,
                preferred_element_type=f32,
            )
        return total

    def reduce_near(stage, target):
        for c in range(3):
            target[c] = gathered(near_recv, stage, 0, c)

    def reduce_far(stage, target, here):
        for c in range(3):
            total = target[c] + gathered(far_recv, stage, 2, c)
            target[c] = total
            if here is not None:
                here[:, c, :] = total

    def mean_of(u, v):
        return jnp.sum(jnp.sum(u * v, axis=0), keepdims=True) * (1.0 / size_all)

    def row_of(values):
        lane_row = lax.broadcasted_iota(i32, (1, lanes), 1)
        row = jnp.zeros((1, lanes), f32)
        for j, value in enumerate(values):
            row = jnp.where(lane_row == j, value, row)
        return row

    def send_sums(values):
        sum_send[0] = row_of(values)
        pltpu.make_async_copy(sum_send.at[0], sum_recv.at[me], recv_sem.at[7]).start()

        def step(peer):
            pltpu.make_async_remote_copy(
                sum_send.at[0],
                sum_recv.at[me],
                send_sem.at[7],
                recv_sem.at[7],
                device_id=(peer,),
                device_id_type=mesh_id,
            ).start()

        every_peer(step)

    def take_sums(count):
        arrived(sum_recv, 7)
        total = jnp.sum(sum_recv[...], axis=0)
        return [total[0:1, j : j + 1] for j in range(count)]

    inner = 16
    outer = n // inner
    position = lax.rem(me, inner)
    group = lax.div(me, inner)

    def group_sum(row, slot, recv, which, own, size, device):
        sum_send[slot] = row
        pltpu.make_async_copy(sum_send.at[slot], recv.at[own], recv_sem.at[which]).start()
        for u in range(1, size):
            pltpu.make_async_remote_copy(
                sum_send.at[slot],
                recv.at[own],
                send_sem.at[which],
                recv_sem.at[which],
                device_id=(device(lax.rem(own + u, size)),),
                device_id_type=mesh_id,
            ).start()
        arrived(recv, which)
        return jnp.sum(recv[...], axis=0)

    def sum_everywhere(values):
        part = group_sum(
            row_of(values), 1, inner_recv, 8, position, inner, lambda i: group * inner + i
        )
        total = group_sum(
            part, 2, outer_recv, 11, group, outer, lambda i: i * inner + position
        )
        return [total[0:1, j : j + 1] for j in range(len(values))]

    spread_first(0, cols_even)
    make_quarter(0, None)
    arrived(x_recv, 2)
    for k in range(1, 4):
        make_quarter(k, x_recv)
    apply_quarter(3, x_recv)
    exchange(near_send.at[0], near_recv.at[0], 4, fill_terms(near_send.at[0], near_terms, 2))
    apply_far(x_recv, 2)
    exchange(far_send.at[0], far_recv.at[0], 3, fill_terms(far_send.at[0], far_terms, 4))
    arrived(near_recv.at[0], 4)
    reduce_near(0, y_all)
    arrived(far_recv.at[0], 3)
    reduce_far(0, y_all, y_here)

    exchange(yn_send, yn_recv, 9, fill_density(yn_send, y_here, (0, 1)))
    exchange(yf_send, yf_recv, 10, fill_density(yf_send, y_here, (2, 3)))
    x = x_ref[...]
    y = y_all[...]
    send_sums([mean_of(x, x), mean_of(x, y), mean_of(y, y)])
    arrived(yn_recv, 9)
    apply_quarter(0, yn_recv)
    apply_quarter(1, yn_recv)
    apply_quarter(2, yn_recv)
    apply_quarter(3, yn_recv)
    exchange(near_send.at[1], near_recv.at[1], 6, fill_terms(near_send.at[1], near_terms, 2))
    arrived(yf_recv, 10)
    apply_far(yf_recv, 0)
    exchange(far_send.at[1], far_recv.at[1], 5, fill_terms(far_send.at[1], far_terms, 4))
    xx, xy, yy = take_sums(3)
    scale_sq = xx + norm_eps
    scale = jnp.sqrt(scale_sq)
    proj_first = xy / scale_sq
    resid_sq = (yy - proj_first * xy * (1.0 + norm_eps / scale_sq)) / scale_sq
    norm_sq = resid_sq + norm_eps
    norm_first = jnp.sqrt(norm_sq)
    shrink = 1.0 / (scale * norm_first)
    x = x_ref[...]
    y = y_all[...]
    basis_one = x / scale
    basis_two = (y - proj_first * x) * shrink
    basis_ref[0] = basis_two
    arrived(near_recv.at[1], 6)
    reduce_near(1, z_all)
    arrived(far_recv.at[1], 5)
    reduce_far(1, z_all, None)
    image_two = (z_all[...] - proj_first * y_all[...]) * shrink
    cross, second, image_sq = sum_everywhere(
        [mean_of(basis_one, image_two), mean_of(basis_two, image_two), mean_of(image_two, image_two)]
    )
    one_sq = xx / scale_sq
    two_sq = resid_sq / norm_sq
    one_two = xy * norm_eps / (scale_sq * scale_sq * norm_first)
    last_sq = (
        image_sq
        + cross * cross * (one_sq - 2.0)
        + second * second * (two_sq - 2.0)
        + 2.0 * cross * second * one_two
    )
    norm_second = jnp.sqrt(last_sq + norm_eps)
    shrink_two = 1.0 / norm_second
    basis_ref[1] = (image_two - cross * basis_one - second * basis_two) * shrink_two
    row_id = lax.broadcasted_iota(i32, (2, 3), 1)
    col_id = lax.broadcasted_iota(i32, (2, 3), 0)
    hess = jnp.zeros((2, 3), f32)
    placed = (
        (0, 0, proj_first),
        (0, 1, cross),
        (1, 0, norm_first),
        (1, 1, second),
        (2, 1, norm_second),
    )
    for r, c, value in placed:
        hess = jnp.where((row_id == r) & (col_id == c), value, hess)
    hess_ref[...] = hess

    sent(req_send, 0)
    sent(geo_send, 1)
    sent(x_send, 2)
    sent(far_send.at[0], 3)
    sent(near_send.at[0], 4)
    sent(far_send.at[1], 5)
    sent(near_send.at[1], 6)
    sent(yn_send, 9)
    sent(yf_send, 10)
    sent(sum_recv, 7, n)
    sent(inner_recv, 8, inner)
    sent(outer_recv, 11, outer)


def per_device(
    right_side, vertices, panels, near_owner, near_local, far_owner, far_local, far_left, far_right
):
    n = lax.axis_size("dev")
    near = near_owner.shape[0]
    far = far_owner.shape[0]
    clusters = right_side.shape[0]

    vmem = pltpu.VMEM
    basis, hess = pl.pallas_call(
        functools.partial(kernel, n, near, far),
        out_shape=(
            jax.ShapeDtypeStruct((2, 3, clusters, lanes), f32),
            jax.ShapeDtypeStruct((2, 3), f32),
        ),
        in_specs=[pl.BlockSpec(memory_space=vmem)] * 9,
        out_specs=(pl.BlockSpec(memory_space=vmem),) * 2,
        scratch_shapes=[
            vmem((n, 1, lanes), f32),
            vmem((n, 1, lanes), f32),
            vmem((8, lanes), i32),
            pltpu.SMEM((8, lanes), i32),
            vmem((8, lanes), i32),
            pltpu.SMEM((8, lanes), i32),
            vmem((4, clusters, lanes), f32),
            vmem((clusters, 3, lanes), f32),
            vmem((clusters, 3, lanes), f32),
            vmem((clusters, 3, lanes), f32),
            vmem((n, 2, 2, 3, lanes), f32),
            vmem((n, 2, 2, 3, lanes), f32),
            vmem((n, 4, 3, lanes), f32),
            vmem((n, 4, 3, lanes), f32),
            vmem((n, 2, 3, lanes), f32),
            vmem((n, 2, 3, lanes), f32),
            vmem((n, 2, 3, lanes), f32),
            vmem((n, 2, 3, lanes), f32),
            vmem((2, n, 2, 3, lanes), f32),
            vmem((2, n, 2, 3, lanes), f32),
            vmem((2, n, 2, 3, lanes), f32),
            vmem((2, n, 2, 3, lanes), f32),
            vmem((near, 4, 8, lanes), f32),
            vmem((32 * near, lanes), f32),
            vmem((near // 4, lanes, lanes), bf16),
            vmem((4, lanes, 9 * lanes), bf16),
            vmem((lanes, 9 * lanes), f32),
            vmem((lanes, 9 * lanes), f32),
            vmem((near // 4, 2 * lanes, 6 * lanes), bf16),
            vmem((near // 4, 2 * lanes, 6 * lanes), bf16),
            vmem((near // 4, 2 * lanes, 6 * lanes), bf16),
            vmem((near // 4, 2 * lanes, 6 * lanes), bf16),
            vmem((4 * lanes + 8, lanes), f32),
            vmem((4 * lanes + 8, lanes), f32),
            vmem((3, clusters, lanes), f32),
            vmem((3, clusters, lanes), f32),
            vmem((clusters, 3, lanes), f32),
            vmem((3, 1, lanes), f32),
            vmem((n, 1, lanes), f32),
            vmem((16, 1, lanes), f32),
            vmem((n // 16, 1, lanes), f32),
            pltpu.SemaphoreType.DMA((12,)),
            pltpu.SemaphoreType.DMA((12,)),
            pltpu.SemaphoreType.DMA((4,)),
        ],
        compiler_params=pltpu.CompilerParams(
            collective_id=0, has_side_effects=True, vmem_limit_bytes=58 * 1024 * 1024
        ),
    )(
        near_owner.T,
        near_local.T,
        far_owner.T,
        far_local.T,
        right_side.transpose(1, 0, 2),
        vertices.transpose(1, 0, 2),
        panels.transpose(1, 0, 2),
        far_left,
        far_right,
    )
    return basis.transpose(0, 2, 1, 3), hess.T


def solution(mesh):
    block = P("dev", None, None)
    pair = P("dev", None)
    return jax.shard_map(
        per_device,
        mesh=mesh,
        in_specs=(block, block, block, pair, pair, pair, pair, block, block),
        out_specs=(P(None, "dev", None, None), P()),
        check_vma=False,
    )
```

```python
import functools

import jax
import jax.numpy as jnp
from jax import lax
from jax.experimental import pallas as pl
from jax.experimental.pallas import tpu as pltpu
from jax.sharding import PartitionSpec as P

highest = lax.Precision.HIGHEST
soft_sq = 0.0025
area_floor = 6.25e-06
kelvin_diag = 1.8
norm_eps = 1e-06
lanes = 128
f32 = jnp.float32
i32 = jnp.int32
bf16 = jnp.bfloat16
mesh_id = pl.DeviceIdType.MESH


def list_tables(owners, locals_, count):
    owner_row = jnp.concatenate([owners[0:1], owners[1:2]], axis=1).astype(f32)
    local_row = jnp.concatenate([locals_[0:1], locals_[1:2]], axis=1).astype(f32)
    shape = (lanes, lanes)
    sub = lax.broadcasted_iota(i32, shape, 0)
    lane = lax.broadcasted_iota(i32, shape, 1)
    tile = (2 * (sub % count) + sub // count - lanes).astype(f32)
    lane_f = lane.astype(f32)
    owner_b = jnp.broadcast_to(owner_row, shape)
    owner_t = owner_b.T
    local_t = jnp.broadcast_to(local_row, shape).T
    same = owner_b == owner_t
    rank_row = jnp.sum(jnp.where(same & (sub < lane), 1.0, 0.0), axis=0, keepdims=True)
    rank_col = jnp.sum(jnp.where(same & (lane < sub), 1.0, 0.0), axis=1, keepdims=True)
    slot_row = owner_row * 2.0 + rank_row
    requests, entries = [], []
    for k in range(2):
        hit = (owner_t == lane_f) & (rank_col == float(k))
        requests.append(jnp.sum(jnp.where(hit, local_t, 0.0), axis=0, keepdims=True))
        entries.append(
            jnp.sum(jnp.where(hit, tile, 0.0), axis=0, keepdims=True) + float(lanes)
        )
    return slot_row, requests, entries


def three_parts(rows):
    high = rows.astype(bf16).astype(f32)
    rest = rows - high
    middle = rest.astype(bf16).astype(f32)
    return [high, middle, rest - middle]


def kernel(
    n,
    near,
    far,
    near_owner_ref,
    near_local_ref,
    far_owner_ref,
    far_local_ref,
    x_ref,
    vert_ref,
    panel_ref,
    left_hbm,
    right_hbm,
    basis_ref,
    hess_ref,
    left_ref,
    right_ref,
    req_send,
    req_recv,
    tab_v,
    tab_s,
    ask_v,
    ask_s,
    one_hot,
    x_here,
    vert_here,
    panel_here,
    geo_send,
    geo_recv,
    x_send,
    x_recv,
    yn_send,
    yn_recv,
    yf_send,
    yf_recv,
    near_send,
    near_recv,
    far_send,
    far_recv,
    points,
    first_rows,
    first_cols,
    picker,
    cols_even,
    cols_odd,
    blocks_0,
    blocks_1,
    blocks_2,
    blocks_3,
    near_terms,
    far_terms,
    y_all,
    z_all,
    y_here,
    sum_send,
    sum_recv,
    inner_recv,
    outer_recv,
    send_sem,
    recv_sem,
    local_sem,
):
    me = lax.axis_index("dev")
    clusters = x_ref.shape[1]
    blocks = (blocks_0, blocks_1, blocks_2, blocks_3)
    size_all = float(clusters * n * 3 * lanes)

    barrier = pltpu.get_barrier_semaphore()

    def every_peer(body):
        group = 4
        count = (n - 1) // group

        def step(g, carry):
            for u in range(group):
                body(lax.rem(me + (1 + group * g + u), n))
            return carry

        lax.fori_loop(0, count, step, 0)
        for i in range(1 + group * count, n):
            body(lax.rem(me + i, n))

    def greet(peer):
        pl.semaphore_signal(barrier, inc=1, device_id=(peer,), device_id_type=mesh_id)

    every_peer(greet)
    left_copy = pltpu.make_async_copy(left_hbm, left_ref, local_sem.at[2])
    right_copy = pltpu.make_async_copy(right_hbm, right_ref, local_sem.at[3])
    left_copy.start()
    right_copy.start()

    def asked_id(k, o):
        return jnp.clip(ask_s[k, o], 0, clusters - 1)

    def entry_slot(row, e):
        slot = jnp.clip(tab_s[row, e], 0, 2 * n - 1)
        return slot >> 1, slot & 1

    near_slot, near_req, near_entry = list_tables(near_owner_ref[...], near_local_ref[...], near)
    far_slot, far_req, far_entry = list_tables(far_owner_ref[...], far_local_ref[...], far)
    rows = [near_slot, far_slot] + near_entry + far_entry
    tab_v[...] = jnp.concatenate(rows + [jnp.zeros((2, lanes), f32)], axis=0).astype(i32)
    to_smem = pltpu.make_async_copy(tab_v, tab_s, local_sem.at[0])
    to_smem.start()
    req_rows = jnp.concatenate(near_req + far_req + [jnp.zeros((lanes - 4, lanes), f32)], axis=0)
    req_send[...] = req_rows.T[:n].reshape(n, 1, lanes)
    pl.semaphore_wait(barrier, n - 1)

    def exchange(send, recv, which, fill):
        fill(me)
        pltpu.make_async_copy(send.at[me], recv.at[me], recv_sem.at[which]).start()

        def step(peer):
            fill(peer)
            pltpu.make_async_remote_copy(
                send.at[peer],
                recv.at[me],
                send_sem.at[which],
                recv_sem.at[which],
                device_id=(peer,),
                device_id_type=mesh_id,
            ).start()

        every_peer(step)

    def arrived(recv, which):
        pltpu.make_async_copy(recv, recv, recv_sem.at[which]).wait()

    def sent(send, which, count=n):
        part = send.at[pl.ds(0, count - 1)]
        pltpu.make_async_copy(part, part, send_sem.at[which]).wait()

    exchange(req_send, req_recv, 0, lambda o: None)
    for c in range(3):
        x_here[:, c, :] = x_ref[c]
        vert_here[:, c, :] = vert_ref[c]
        panel_here[:, c, :] = panel_ref[c].astype(f32)
    near_terms[pl.ds(4 * lanes, 8), :] = jnp.zeros((8, lanes), f32)
    far_terms[pl.ds(4 * lanes, 8), :] = jnp.zeros((8, lanes), f32)

    picked = lax.broadcasted_iota(i32, (lanes, lanes), 0)
    for r in range(4):
        for j in range(9):
            place = picked - 32 * r
            if j < 8:
                hit = (place == j) | (place == 8 + j) | (place == 16 + j)
            else:
                hit = (place >= 24) & (place < 27)
            picker[r, :, pl.ds(j * lanes, lanes)] = jnp.where(hit, 1.0, 0.0).astype(bf16)

    arrived(req_recv, 0)
    asked = req_recv[...].reshape(n, lanes)
    if n < lanes:
        asked = jnp.concatenate([asked, jnp.zeros((lanes - n, lanes), f32)], axis=0)
    asked = asked.T
    ask_v[...] = asked[0:8].astype(i32)
    ask_copy = pltpu.make_async_copy(ask_v, ask_s, local_sem.at[1])
    ask_copy.start()
    cluster_ids = lax.broadcasted_iota(i32, (clusters, lanes), 0).astype(f32)
    for k in range(4):
        one_hot[k] = jnp.where(cluster_ids == asked[k : k + 1], 1.0, 0.0)
    ask_copy.wait()
    to_smem.wait()

    def fill_geo(o):
        for k in range(2):
            c = asked_id(k, o)
            geo_send[o, k, 0] = vert_here[c]
            geo_send[o, k, 1] = panel_here[c]

    def fill_density(send, source, slots):
        def fill(o):
            for j, k in enumerate(slots):
                send[o, j] = source[asked_id(k, o)]

        return fill

    exchange(geo_send, geo_recv, 1, fill_geo)
    exchange(x_send, x_recv, 2, fill_density(x_send, x_here, (0, 1, 2, 3)))
    arrived(geo_recv, 1)

    def make_points(p):
        owner_a, rank_a = entry_slot(0, p)
        owner_b, rank_b = entry_slot(0, near + p)
        va = geo_recv[owner_a, rank_a, 0]
        vb = geo_recv[owner_b, rank_b, 0]
        pa = geo_recv[owner_a, rank_a, 1].astype(i32)
        pb = geo_recv[owner_b, rank_b, 1].astype(i32)
        table = jnp.concatenate([va, va[0:1], vb, vb[0:1]], axis=0)
        corners = []
        for m in range(3):
            picks = jnp.concatenate(
                [
                    jnp.broadcast_to(pa[m : m + 1], (4, lanes)),
                    jnp.broadcast_to(pb[m : m + 1], (4, lanes)),
                ],
                axis=0,
            )
            corners.append(
                jnp.take_along_axis(table, picks, axis=1, mode="promise_in_bounds")
            )
        edge_one = corners[1] - corners[0]
        edge_two = corners[2] - corners[0]
        cross = edge_one * pltpu.roll(edge_two, 7, 0) - pltpu.roll(edge_one, 7, 0) * edge_two
        squares = cross * cross
        area = squares + pltpu.roll(squares, 7, 0) + pltpu.roll(squares, 6, 0)
        weight = jnp.sqrt(area + area_floor) / 6.0
        for s in range(3):
            others = [corners[m] for m in range(3) if m != s]
            points[p, s] = (2.0 / 3.0) * corners[s] + (1.0 / 6.0) * (others[0] + others[1])
        points[p, 3] = weight
        firsts = [points[p, s] for s in range(3)]
        head = jnp.concatenate([firsts[0][0:3], firsts[1][0:3], firsts[2][0:2]], axis=0)
        head_parts, tail_parts = three_parts(head), three_parts(firsts[2])
        first_rows[pl.ds(pl.multiple_of(32 * p, 32), 32), :] = jnp.concatenate(
            head_parts + [part[2:3] for part in tail_parts] + [jnp.zeros((5, lanes), f32)], axis=0
        )

    def points_step(h, carry):
        for u in range(4):
            make_points(4 * h + u)
        return carry

    lax.fori_loop(0, near // 4, points_step, 0)

    def turn_points(g, carry):
        rows = first_rows[pl.ds(pl.multiple_of(lanes * g, lanes), lanes), :]
        first_cols[g] = rows.T.astype(bf16)
        return carry

    lax.fori_loop(0, near // 4, turn_points, 0)

    chunk = 16

    def spread_first(p, target):
        target[...] = jnp.dot(first_cols[p // 4], picker[p % 4], preferred_element_type=f32)

    def make_block(p, cols, target, at):
        for c in range(lanes // chunk):
            at_rows = pl.ds(c * chunk, chunk)
            sums = None
            for s in range(3):
                a = [cols[at_rows, pl.ds((3 * s + i) * lanes, lanes)] for i in range(3)]
                for t in range(3):
                    d = [a[i] - points[p, t, 4 + i : 5 + i, :] for i in range(3)]
                    inv = lax.rsqrt(d[0] * d[0] + d[1] * d[1] + (d[2] * d[2] + soft_sq))
                    cube = inv * inv * inv
                    e0 = cube * d[0]
                    e1 = cube * d[1]
                    terms = [inv, cube, e0 * d[0], e0 * d[1], e0 * d[2], e1 * d[1], e1 * d[2]]
                    if sums is None:
                        sums = terms
                    else:
                        sums = [total + term for total, term in zip(sums, terms)]
            inv_sum, cube_sum, *outer = sums
            last = inv_sum - soft_sq * cube_sum - outer[0] - outer[3]
            diag = kelvin_diag * inv_sum
            entries = (
                outer[0] + diag,
                outer[1],
                outer[2],
                outer[3] + diag,
                outer[4],
                last + diag,
            )
            for q in range(6):
                value = entries[q]
                high = value.astype(bf16)
                at_lanes = pl.ds(q * lanes, lanes)
                target[at, at_rows, at_lanes] = high
                target[at, pl.ds(lanes + c * chunk, chunk), at_lanes] = (
                    value - high.astype(f32)
                ).astype(bf16)

    quarter = near // 4

    def make_quarter(k, recv):
        def step(h, carry):
            at = 2 * h
            p = k * quarter + at
            spread_first(p + 1, cols_odd)
            if recv is not None:
                near_pair(recv, p - quarter, blocks[k - 1], at)
            make_block(p, cols_even, blocks[k], at)
            spread_first(jnp.minimum(p + 2, near - 1), cols_even)
            if recv is not None:
                near_pair(recv, p + 1 - quarter, blocks[k - 1], at + 1)
            make_block(p + 1, cols_odd, blocks[k], at + 1)
            return carry

        lax.fori_loop(0, quarter // 2, step, 0)

    def apply_far(recv, base):
        def one(f):
            owner_a, rank_a = entry_slot(1, f)
            owner_b, rank_b = entry_slot(1, far + f)
            xa = recv[owner_a, base + rank_a]
            xb = recv[owner_b, base + rank_b]
            left = [left_ref[f, :, pl.ds(c * lanes, lanes)] for c in range(3)]
            right = [right_ref[f, :, pl.ds(c * lanes, lanes)] for c in range(3)]
            coef_b = jnp.sum(
                right[0] * xb[0:1] + right[1] * xb[1:2] + right[2] * xb[2:3], axis=1, keepdims=True
            )
            coef_a = jnp.sum(
                left[0] * xa[0:1] + left[1] * xa[1:2] + left[2] * xa[2:3], axis=1, keepdims=True
            )
            for c in range(3):
                far_terms[pl.ds(8 * f + c, 1), :] = jnp.sum(left[c] * coef_b, axis=0, keepdims=True)
                far_terms[pl.ds(8 * f + 4 + c, 1), :] = jnp.sum(
                    right[c] * coef_a, axis=0, keepdims=True
                )

        def step(h, carry):
            for u in range(4):
                one(4 * h + u)
            return carry

        lax.fori_loop(0, far // 4, step, 0)

    places = (
        ((0, 0),),
        ((0, 1), (1, 0)),
        ((0, 2), (2, 0)),
        ((1, 1),),
        ((1, 2), (2, 1)),
        ((2, 2),),
    )
    sub_id = lax.broadcasted_iota(i32, (8, lanes), 0)
    comp = sub_id % 4

    def spread_density(rows):
        split = []
        for i in range(3):
            row = rows[i : i + 1]
            high = row.astype(bf16).astype(f32)
            split.append(jnp.where(sub_id < 4, high, row - high))
        empty = jnp.zeros((8, lanes), f32)
        out = []
        for place in places:
            value = empty
            for r, i in place:
                value = jnp.where(comp == r, split[i], value)
            out.append(jnp.concatenate([value, empty], axis=0).astype(bf16))
        return out

    def near_pair(recv, p, block, at):
        owner_a, rank_a = entry_slot(0, p)
        owner_b, rank_b = entry_slot(0, near + p)
        weight_a = points[p, 3, 0:1, :]
        weight_b = points[p, 3, 4:5, :]
        a = spread_density(recv[owner_a, rank_a] * weight_a)
        b = spread_density(recv[owner_b, rank_b] * weight_b)
        into_b = jnp.zeros((8, lanes), f32)
        for q in range(6):
            into_b = into_b + jnp.dot(
                jnp.concatenate([a[q], a[q]], axis=1),
                block[at, :, pl.ds(q * lanes, lanes)],
                preferred_element_type=f32,
            )[0:8]
        back = lax.dot_general(
            jnp.concatenate(b, axis=1),
            block[at],
            (((1,), (1,)), ((), ())),
            preferred_element_type=f32,
        )
        into_a = back[0:8, :lanes] + back[0:8, lanes:]
        into_a = (into_a + pltpu.roll(into_a, 4, 0)) * weight_a
        into_b = (into_b + pltpu.roll(into_b, 4, 0)) * weight_b
        near_terms[pl.ds(pl.multiple_of(8 * p, 8), 8), :] = jnp.where(sub_id < 4, into_a, into_b)

    def apply_quarter(k, recv):
        def step(h, carry):
            for u in range(4):
                near_pair(recv, k * quarter + 4 * h + u, blocks[k], 4 * h + u)
            return carry

        lax.fori_loop(0, quarter // 4, step, 0)

    def fill_terms(send, source, row):
        def fill(o):
            for k in range(2):
                entry = jnp.clip(tab_s[row + k, o], 0, lanes)
                send[o, k] = source[pl.ds(4 * entry, 3), :]

        return fill

    def gathered(recv, stage, first, c):
        total = jnp.zeros((clusters, lanes), f32)
        for k in range(2):
            total = total + jnp.dot(
                one_hot[first + k, :, pl.ds(0, n)],
                recv[stage, :, k, c, :],
                precision=highest,
                preferred_element_type=f32,
            )
        return total

    def reduce_far(stage, target):
        for c in range(3):
            target[c] = gathered(far_recv, stage, 2, c)

    def reduce_near(stage, target, here):
        for c in range(3):
            total = target[c] + gathered(near_recv, stage, 0, c)
            target[c] = total
            if here is not None:
                here[:, c, :] = total

    def mean_of(u, v):
        return jnp.sum(jnp.sum(u * v, axis=0), keepdims=True) * (1.0 / size_all)

    def row_of(values):
        lane_row = lax.broadcasted_iota(i32, (1, lanes), 1)
        row = jnp.zeros((1, lanes), f32)
        for j, value in enumerate(values):
            row = jnp.where(lane_row == j, value, row)
        return row

    def send_sums(values):
        sum_send[0] = row_of(values)
        pltpu.make_async_copy(sum_send.at[0], sum_recv.at[me], recv_sem.at[7]).start()

        def step(peer):
            pltpu.make_async_remote_copy(
                sum_send.at[0],
                sum_recv.at[me],
                send_sem.at[7],
                recv_sem.at[7],
                device_id=(peer,),
                device_id_type=mesh_id,
            ).start()

        every_peer(step)

    def take_sums(count):
        arrived(sum_recv, 7)
        total = jnp.sum(sum_recv[...], axis=0)
        return [total[0:1, j : j + 1] for j in range(count)]

    inner = 16
    outer = n // inner
    position = lax.rem(me, inner)
    group = lax.div(me, inner)

    def group_sum(row, slot, recv, which, own, size, device):
        sum_send[slot] = row
        pltpu.make_async_copy(sum_send.at[slot], recv.at[own], recv_sem.at[which]).start()
        for u in range(1, size):
            pltpu.make_async_remote_copy(
                sum_send.at[slot],
                recv.at[own],
                send_sem.at[which],
                recv_sem.at[which],
                device_id=(device(lax.rem(own + u, size)),),
                device_id_type=mesh_id,
            ).start()
        arrived(recv, which)
        return jnp.sum(recv[...], axis=0)

    def sum_everywhere(values):
        part = group_sum(
            row_of(values), 1, inner_recv, 8, position, inner, lambda i: group * inner + i
        )
        total = group_sum(
            part, 2, outer_recv, 11, group, outer, lambda i: i * inner + position
        )
        return [total[0:1, j : j + 1] for j in range(len(values))]

    spread_first(0, cols_even)
    make_quarter(0, None)
    arrived(x_recv, 2)
    left_copy.wait()
    right_copy.wait()
    apply_far(x_recv, 2)
    exchange(far_send.at[0], far_recv.at[0], 3, fill_terms(far_send.at[0], far_terms, 4))
    for k in range(1, 4):
        make_quarter(k, x_recv)
    apply_quarter(3, x_recv)
    exchange(near_send.at[0], near_recv.at[0], 4, fill_terms(near_send.at[0], near_terms, 2))
    arrived(far_recv.at[0], 3)
    reduce_far(0, y_all)
    arrived(near_recv.at[0], 4)
    reduce_near(0, y_all, y_here)

    exchange(yn_send, yn_recv, 9, fill_density(yn_send, y_here, (0, 1)))
    exchange(yf_send, yf_recv, 10, fill_density(yf_send, y_here, (2, 3)))
    x = x_ref[...]
    y = y_all[...]
    send_sums([mean_of(x, x), mean_of(x, y), mean_of(y, y)])
    arrived(yn_recv, 9)
    apply_quarter(0, yn_recv)
    apply_quarter(1, yn_recv)
    arrived(yf_recv, 10)
    apply_far(yf_recv, 0)
    exchange(far_send.at[1], far_recv.at[1], 5, fill_terms(far_send.at[1], far_terms, 4))
    apply_quarter(2, yn_recv)
    apply_quarter(3, yn_recv)
    exchange(near_send.at[1], near_recv.at[1], 6, fill_terms(near_send.at[1], near_terms, 2))
    xx, xy, yy = take_sums(3)
    scale_sq = xx + norm_eps
    scale = jnp.sqrt(scale_sq)
    proj_first = xy / scale_sq
    resid_sq = (yy - proj_first * xy * (1.0 + norm_eps / scale_sq)) / scale_sq
    norm_sq = resid_sq + norm_eps
    norm_first = jnp.sqrt(norm_sq)
    shrink = 1.0 / (scale * norm_first)
    x = x_ref[...]
    y = y_all[...]
    basis_one = x / scale
    basis_two = (y - proj_first * x) * shrink
    basis_ref[0] = basis_two
    arrived(far_recv.at[1], 5)
    reduce_far(1, z_all)
    arrived(near_recv.at[1], 6)
    reduce_near(1, z_all, None)
    image_two = (z_all[...] - proj_first * y_all[...]) * shrink
    cross, second, image_sq = sum_everywhere(
        [mean_of(basis_one, image_two), mean_of(basis_two, image_two), mean_of(image_two, image_two)]
    )
    one_sq = xx / scale_sq
    two_sq = resid_sq / norm_sq
    one_two = xy * norm_eps / (scale_sq * scale_sq * norm_first)
    last_sq = (
        image_sq
        + cross * cross * (one_sq - 2.0)
        + second * second * (two_sq - 2.0)
        + 2.0 * cross * second * one_two
    )
    norm_second = jnp.sqrt(last_sq + norm_eps)
    shrink_two = 1.0 / norm_second
    basis_ref[1] = (image_two - cross * basis_one - second * basis_two) * shrink_two
    row_id = lax.broadcasted_iota(i32, (2, 3), 1)
    col_id = lax.broadcasted_iota(i32, (2, 3), 0)
    hess = jnp.zeros((2, 3), f32)
    placed = (
        (0, 0, proj_first),
        (0, 1, cross),
        (1, 0, norm_first),
        (1, 1, second),
        (2, 1, norm_second),
    )
    for r, c, value in placed:
        hess = jnp.where((row_id == r) & (col_id == c), value, hess)
    hess_ref[...] = hess

    sent(req_send, 0)
    sent(geo_send, 1)
    sent(x_send, 2)
    sent(far_send.at[0], 3)
    sent(near_send.at[0], 4)
    sent(far_send.at[1], 5)
    sent(near_send.at[1], 6)
    sent(yn_send, 9)
    sent(yf_send, 10)
    sent(sum_recv, 7, n)
    sent(inner_recv, 8, inner)
    sent(outer_recv, 11, outer)


def per_device(
    right_side, vertices, panels, near_owner, near_local, far_owner, far_local, far_left, far_right
):
    n = lax.axis_size("dev")
    near = near_owner.shape[0]
    far = far_owner.shape[0]
    clusters = right_side.shape[0]

    vmem = pltpu.VMEM
    basis, hess = pl.pallas_call(
        functools.partial(kernel, n, near, far),
        out_shape=(
            jax.ShapeDtypeStruct((2, 3, clusters, lanes), f32),
            jax.ShapeDtypeStruct((2, 3), f32),
        ),
        in_specs=[pl.BlockSpec(memory_space=vmem)] * 7
        + [pl.BlockSpec(memory_space=pl.ANY)] * 2,
        out_specs=(pl.BlockSpec(memory_space=vmem),) * 2,
        scratch_shapes=[
            vmem(far_left.shape, f32),
            vmem(far_right.shape, f32),
            vmem((n, 1, lanes), f32),
            vmem((n, 1, lanes), f32),
            vmem((8, lanes), i32),
            pltpu.SMEM((8, lanes), i32),
            vmem((8, lanes), i32),
            pltpu.SMEM((8, lanes), i32),
            vmem((4, clusters, lanes), f32),
            vmem((clusters, 3, lanes), f32),
            vmem((clusters, 3, lanes), f32),
            vmem((clusters, 3, lanes), f32),
            vmem((n, 2, 2, 3, lanes), f32),
            vmem((n, 2, 2, 3, lanes), f32),
            vmem((n, 4, 3, lanes), f32),
            vmem((n, 4, 3, lanes), f32),
            vmem((n, 2, 3, lanes), f32),
            vmem((n, 2, 3, lanes), f32),
            vmem((n, 2, 3, lanes), f32),
            vmem((n, 2, 3, lanes), f32),
            vmem((2, n, 2, 3, lanes), f32),
            vmem((2, n, 2, 3, lanes), f32),
            vmem((2, n, 2, 3, lanes), f32),
            vmem((2, n, 2, 3, lanes), f32),
            vmem((near, 4, 8, lanes), f32),
            vmem((32 * near, lanes), f32),
            vmem((near // 4, lanes, lanes), bf16),
            vmem((4, lanes, 9 * lanes), bf16),
            vmem((lanes, 9 * lanes), f32),
            vmem((lanes, 9 * lanes), f32),
            vmem((near // 4, 2 * lanes, 6 * lanes), bf16),
            vmem((near // 4, 2 * lanes, 6 * lanes), bf16),
            vmem((near // 4, 2 * lanes, 6 * lanes), bf16),
            vmem((near // 4, 2 * lanes, 6 * lanes), bf16),
            vmem((4 * lanes + 8, lanes), f32),
            vmem((4 * lanes + 8, lanes), f32),
            vmem((3, clusters, lanes), f32),
            vmem((3, clusters, lanes), f32),
            vmem((clusters, 3, lanes), f32),
            vmem((3, 1, lanes), f32),
            vmem((n, 1, lanes), f32),
            vmem((16, 1, lanes), f32),
            vmem((n // 16, 1, lanes), f32),
            pltpu.SemaphoreType.DMA((12,)),
            pltpu.SemaphoreType.DMA((12,)),
            pltpu.SemaphoreType.DMA((4,)),
        ],
        compiler_params=pltpu.CompilerParams(
            collective_id=0, has_side_effects=True, vmem_limit_bytes=58 * 1024 * 1024
        ),
    )(
        near_owner.T,
        near_local.T,
        far_owner.T,
        far_local.T,
        right_side.transpose(1, 0, 2),
        vertices.transpose(1, 0, 2),
        panels.transpose(1, 0, 2),
        far_left,
        far_right,
    )
    return basis.transpose(0, 2, 1, 3), hess.T


def solution(mesh):
    block = P("dev", None, None)
    pair = P("dev", None)
    return jax.shard_map(
        per_device,
        mesh=mesh,
        in_specs=(block, block, block, pair, pair, pair, pair, block, block),
        out_specs=(P(None, "dev", None, None), P()),
        check_vma=False,
    )
```
